512 devices in a mesh: row: 16 (over z_lo, y), col: 32 (over z_hi, x, core).
Axes of the slice: x: 4, y: 4, z: 16 (z_hi: 4, z_lo: 4; z = z_hi * 4 + z_lo), core: 2. Of those that a mesh axis runs over, the one named last changes fastest.
Arguments:
- contact_map: bfloat16 [1024, 1024, 128], P('row', 'col'), may hold values from -6 to 6
- cotangent: bfloat16 [1024, 1024, 128], P('row', 'col'), may hold values from -6 to 6
- conv_weight: bfloat16 [3, 3, 3, 128, 128], replicated, may hold values from -0.1875 to 0.1875
- proj_weight: bfloat16 [3, 128, 128], replicated, may hold values from -0.5 to 0.5
Outputs:
- map_grad: bfloat16 [1024, 1024, 128], P('row', 'col')
- conv_grad: float32 [3, 3, 3, 128, 128], replicated
- proj_grad: float32 [3, 128, 128], replicated
The draws below stay inside these ranges and needn't reach their ends.
All inputs are finite; a program needn't handle non-finite values.
Results may differ from the reference program's by a relative error of at most 0.019.
Values may be sent and summed in bfloat16 or wider, within the bound.
A program may use at most 64 MiB of HBM per device.

```python
import jax
import jax.numpy as jnp
from jax import lax

CH = 128
BLOCKS = 3
BINS = 1024


def block_scale(key, dims, pieces, low, largest):
    def one(position, shards_of):
        heights = jax.random.uniform(jax.random.fold_in(jax.random.fold_in(key, 6), position), (shards_of,), jnp.float32, low / len(pieces), largest / len(pieces))
        return jnp.repeat(jnp.exp(heights), dims[position] // shards_of).reshape((-1,) + (1,) * (len(dims) - position - 1))

    loudness = one(*pieces[0])
    for cut in pieces[1:]:
        loudness = loudness * one(*cut)
    return loudness


def scatter_about(stream_key, dims, deviation, bound, cuts=(), kind=jnp.bfloat16):
    factor_of = block_scale(stream_key, dims, cuts, -0.22, 0.18) if cuts else 1.0
    values = jax.random.normal(stream_key, dims, jnp.float32) * deviation * factor_of
    return jnp.minimum(jnp.maximum(values, -bound), bound).astype(kind)


def setup_inputs(seed: int = 0) -> dict:
    streams_of = jax.random.split(jax.random.key(seed), 5)
    return {
        "contact_map": scatter_about(streams_of[0], (BINS, BINS, CH), 1.0, 6.0, ((0, 16), (1, 32))),
        "cotangent": scatter_about(streams_of[1], (BINS, BINS, CH), 1.0, 6.0, ((0, 16), (1, 32))),
        "conv_weight": scatter_about(streams_of[2], (BLOCKS, 3, 3, CH, CH), (9 * CH) ** -0.5, 0.1875),
        "proj_weight": scatter_about(streams_of[3], (BLOCKS, CH, CH), CH ** -0.5, 0.5),
    }


def rounded(values):
    return lax.optimization_barrier(values.astype(jnp.bfloat16))

def gelu_slope(values):
    return jax.vjp(jax.nn.gelu, values)[1](jnp.ones_like(values))[0]

def dilated(field_in, kernel, dilation):
    return lax.conv_general_dilated(field_in[None], kernel, (1, 1), ((dilation, dilation), (dilation, dilation)), rhs_dilation=(dilation, dilation), dimension_numbers=('NHWC', 'HWIO', 'NHWC'), precision=lax.Precision.HIGHEST)[0]

def forward_block(hidden, kernel, projection, dilation):
    activated = rounded(jax.nn.gelu(hidden.astype(jnp.float32)))
    summed = dilated(activated.astype(jnp.float32), kernel.astype(jnp.float32), dilation)
    middle = rounded(jax.nn.gelu(summed))
    branch = jnp.einsum('ijc,cd->ijd', middle.astype(jnp.float32), projection.astype(jnp.float32), precision=lax.Precision.HIGHEST)
    return (activated, summed, middle, branch)

def reference(contact_map, cotangent, conv_weight, proj_weight):
    map_bins = contact_map.shape[0]
    block_count = conv_weight.shape[0]
    flipped = jnp.swapaxes(contact_map, 0, 1)
    hidden = rounded(0.5 * (contact_map.astype(jnp.float32) + flipped.astype(jnp.float32)))
    states = [hidden]
    for block_index in range(block_count - 1):
        branch = forward_block(hidden, conv_weight[block_index], proj_weight[block_index], 2 ** (block_index + 1))[3]
        hidden = rounded(hidden.astype(jnp.float32) + branch)
        states.append(hidden)
    gradient = cotangent
    conv_grads = []
    proj_grads = []
    for block_index in reversed(range(block_count)):
        dilation = 2 ** (block_index + 1)
        activated, summed, middle, branch = forward_block(states[block_index], conv_weight[block_index], proj_weight[block_index], dilation)
        grad_wide = gradient.astype(jnp.float32)
        back_middle = jnp.einsum('ijd,cd->ijc', grad_wide, proj_weight[block_index].astype(jnp.float32), precision=lax.Precision.HIGHEST)
        back_summed = rounded(back_middle * gelu_slope(summed))
        proj_grads.append(jnp.einsum('ijc,ijd->cd', middle.astype(jnp.float32), grad_wide, precision=lax.Precision.HIGHEST) / map_bins)
        padded = jnp.pad(activated.astype(jnp.float32), ((dilation, dilation), (dilation, dilation), (0, 0)))
        back_wide = back_summed.astype(jnp.float32)
        tap_terms = []
        for tap_row in range(3):
            for tap_col in range(3):
                window = padded[tap_row * dilation:tap_row * dilation + map_bins, tap_col * dilation:tap_col * dilation + map_bins]
                tap_terms.append(jnp.einsum('ijc,ijd->cd', window, back_wide, precision=lax.Precision.HIGHEST))
        conv_grads.append(jnp.stack(tap_terms).reshape(3, 3, tap_terms[0].shape[0], tap_terms[0].shape[1]) / map_bins)
        flipped_kernel = jnp.swapaxes(conv_weight[block_index][::-1, ::-1], 2, 3).astype(jnp.float32)
        back_act = dilated(back_wide, flipped_kernel, dilation)
        gradient = rounded(grad_wide + back_act * gelu_slope(states[block_index].astype(jnp.float32)))
    grad_float = gradient.astype(jnp.float32)
    map_grad = (0.5 * (grad_float + jnp.swapaxes(grad_float, 0, 1))).astype(jnp.bfloat16)
    return (map_grad, jnp.stack(conv_grads[::-1]), jnp.stack(proj_grads[::-1]))
```

```python
import functools

import jax
import jax.numpy as jnp
from jax import lax
from jax.experimental import pallas as pl
from jax.experimental.pallas import tpu as pltpu
from jax.sharding import PartitionSpec as P

MESH = pl.DeviceIdType.MESH
BF = jnp.bfloat16
F32 = jnp.float32
ROWS, COLS, CH, MARGIN = 64, 32, 128, 8
CELLS = ROWS * COLS
HIGH, WIDE = ROWS + 2 * MARGIN, COLS + 2 * MARGIN
STEP = 8
CHUNK = STEP * COLS
CHUNKS = ROWS // STEP
TAPS = 9
BLOCKS = 3
SLOPE_C = 0.7978845608028654
CUBIC = 0.044715
MOVES = ((0, -1), (0, 1), (-1, 0), (1, 0), (-1, -1), (-1, 1), (1, -1), (1, 1))
GROUPS = ((2, 1), (0,))
BLOCK_ROWS = (TAPS + 1) * CH


def gelu_parts(v):
    u = v * v
    t = jnp.tanh(SLOPE_C * v * (1.0 + CUBIC * u))
    half = 0.5 + 0.5 * t
    slope = half + (0.5 * SLOPE_C) * v * (1.0 - t * t) * (1.0 + 3.0 * CUBIC * u)
    return v * half, slope


def dot(a, b):
    return jnp.dot(a, b, preferred_element_type=F32)


def dot_nt(a, b):
    return lax.dot_general(a, b, (((1,), (1,)), ((), ())), preferred_element_type=F32)


def dot_tn(a, b):
    return lax.dot_general(a, b, (((0,), (0,)), ((), ())), preferred_element_type=F32)


class Place:
    def __init__(self, rows, cols):
        self.rows, self.cols = rows, cols
        self.side = 4 if rows >= 16 else 2
        self.depth = (rows // self.side) * (cols // (2 * self.side))
        self.parts = rows // self.side
        self.r, self.c = lax.axis_index("row"), lax.axis_index("col")
        self.y, self.zl = self.r % self.side, self.r // self.side
        self.k = self.c % 2
        self.q = self.c // 2
        self.x, self.zh = self.q % self.side, self.q // self.side
        self.z = self.zh * self.parts + self.zl

    def at_core(self):
        return (self.r, self.c + 1 - 2 * self.k)

    def at_x(self, offset):
        x = (self.x + offset) % self.side
        return (self.r, self.zh * 2 * self.side + 2 * x + self.k)

    def at_y(self, offset):
        y = (self.y + offset) % self.side
        return (self.zl * self.side + y, self.c)

    def at_z(self, z):
        zh, zl = z // self.parts, z % self.parts
        return (zl * self.side + self.y, zh * 2 * self.side + 2 * self.x + self.k)

    def inside(self, dr, dc):
        r, c = self.r + dr, self.c + dc
        return (r >= 0) & (r < self.rows) & (c >= 0) & (c < self.cols)


class Sent:
    def __init__(self):
        self.items = []

    def start(self, cond, copy):
        if cond is None:
            copy.start()
        else:
            pl.when(cond)(copy.start)
        self.items.append((cond, copy))

    def finish(self):
        for cond, copy in self.items:
            if cond is None:
                copy.wait_send()
            else:
                pl.when(cond)(copy.wait_send)


def remote(src, dst, send, recv, device):
    return pltpu.make_async_remote_copy(
        src_ref=src, dst_ref=dst, send_sem=send, recv_sem=recv, device_id=device, device_id_type=MESH
    )


class Reduce:
    @staticmethod
    def sizes(n, side, depth):
        half = n // 2
        xq = half // side
        yq = xq // side
        tiles = yq // 8
        zr = 8 * -(-tiles // depth)
        return half, xq, yq, zr

    @staticmethod
    def scratch(n, side, depth):
        half, xq, yq, zr = Reduce.sizes(n, side, depth)
        dma = pltpu.SemaphoreType.DMA
        return [
            pltpu.VMEM((n, CH), BF),
            pltpu.VMEM((half, CH), BF),
            pltpu.VMEM((half, CH), BF),
            pltpu.VMEM((side - 1, xq, CH), BF),
            pltpu.VMEM((xq, CH), F32),
            pltpu.VMEM((side - 1, yq, CH), F32),
            pltpu.VMEM((yq, CH), F32),
            pltpu.VMEM((depth, zr, CH), F32),
            pltpu.VMEM((yq, CH), F32),
            pltpu.VMEM((xq, CH), F32),
            pltpu.VMEM((xq, CH), BF),
            pltpu.VMEM((half, CH), BF),
            pltpu.VMEM((n, CH), BF),
            dma((4, 4)),
            dma((4, 4)),
            dma((4,)),
            dma((4,)),
            dma((2, depth)),
            dma((2, depth)),
        ]

    def __init__(self, n, place, sent, refs):
        self.n, self.p, self.sent = n, place, sent
        self.half, self.xq, self.yq, self.zr = Reduce.sizes(n, place.side, place.depth)
        self.owners = self.yq // self.zr
        (self.src, self.rc, self.s1, self.rx, self.s2, self.ry, self.s3, self.rz, self.g3, self.g2,
         self.g2b, self.g1, self.fin, self.ssem, self.rsem, self.csend, self.crecv, self.zsend,
         self.zrecv) = refs
        self.waits = []

    def rows(self, index, size):
        return pl.ds(pl.multiple_of(index * size, 8), size)

    def rows16(self, index, size):
        return pl.ds(pl.multiple_of(index * size, 16), size)

    def _wait(self):
        for copy in self.waits:
            copy.wait_recv()
        self.waits = []

    def _send(self, src, dst, send, recv, device):
        copy = remote(src, dst, send, recv, device)
        self.sent.start(None, copy)
        self.waits.append(copy)

    def core_start(self):
        p = self.p
        self._send(self.src.at[self.rows16(1 - p.k, self.half)], self.rc, self.csend.at[0], self.crecv.at[0], p.at_core())

    def core_add(self):
        self._wait()
        own = self.rows16(self.p.k, self.half)
        self.s1[...] = (self.src[own, :].astype(F32) + self.rc[...].astype(F32)).astype(BF)

    def x_start(self):
        p = self.p
        for o in range(1, p.side):
            other = (p.x + o) % p.side
            self._send(self.s1.at[self.rows16(other, self.xq)], self.rx.at[o - 1], self.ssem.at[0, o], self.rsem.at[0, o], p.at_x(o))

    def x_add(self):
        self._wait()
        total = self.s1[self.rows16(self.p.x, self.xq), :].astype(F32)
        for o in range(1, self.p.side):
            total = total + self.rx[o - 1].astype(F32)
        self.s2[...] = total

    def y_start(self):
        p = self.p
        for o in range(1, p.side):
            other = (p.y + o) % p.side
            self._send(self.s2.at[self.rows(other, self.yq)], self.ry.at[o - 1], self.ssem.at[1, o], self.rsem.at[1, o], p.at_y(o))

    def y_add(self):
        self._wait()
        total = self.s2[self.rows(self.p.y, self.yq), :]
        for o in range(1, self.p.side):
            total = total + self.ry[o - 1]
        self.s3[...] = total

    def _z_out(self, o):
        p = self.p
        z = (p.z + o) % p.depth
        return z, remote(self.s3.at[self.rows(z, self.zr)], self.rz.at[o], self.zsend.at[0, o], self.zrecv.at[0, o], p.at_z(z))

    def z_start(self):
        def body(o, _):
            z = (self.p.z + o) % self.p.depth

            @pl.when(z < self.owners)
            def _():
                self._z_out(o)[1].start()

            return 0

        lax.fori_loop(1, self.p.depth, body, 0)

    def z_add(self):
        p = self.p

        @pl.when(p.z < self.owners)
        def _():
            def wait(o, _):
                remote(self.rz.at[o], self.rz.at[o], self.zsend.at[0, o], self.zrecv.at[0, o], p.at_z(p.z)).wait_recv()
                return 0

            lax.fori_loop(1, p.depth, wait, 0)
            own = self.rows(p.z, self.zr)
            total = self.s3[own, :]
            for o in range(1, p.depth):
                total = total + self.rz[o]
            self.g3[own, :] = total

    def _z_back(self, o):
        p = self.p
        z = (p.z + o) % p.depth
        own = self.g3.at[self.rows(p.z, self.zr)]
        return remote(own, own, self.zsend.at[1, o], self.zrecv.at[1, p.z], p.at_z(z))

    def zg_start(self):
        p = self.p

        @pl.when(p.z < self.owners)
        def _():
            def body(o, _):
                self._z_back(o).start()
                return 0

            lax.fori_loop(1, p.depth, body, 0)

    def zg_wait(self):
        p = self.p

        def body(z, _):
            @pl.when(z != p.z)
            def _():
                part = self.g3.at[self.rows(z, self.zr)]
                remote(part, part, self.zsend.at[1, z], self.zrecv.at[1, z], p.at_z(z)).wait_recv()

            return 0

        lax.fori_loop(0, self.owners, body, 0)

    def yg_start(self):
        p = self.p
        own = self.rows(p.y, self.yq)
        for o in range(1, p.side):
            copy = remote(self.g3, self.g2.at[own], self.ssem.at[2, o], self.rsem.at[2, o], p.at_y(o))
            self.sent.start(None, copy)
            other = self.rows((p.y + p.side - o) % p.side, self.yq)
            self.waits.append(remote(self.g3, self.g2.at[other], self.ssem.at[2, o], self.rsem.at[2, o], p.at_y(o)))
        self.g2[own, :] = self.g3[...]

    def xg_start(self):
        self._wait()
        p = self.p
        self.g2b[...] = self.g2[...].astype(BF)
        own = self.rows16(p.x, self.xq)
        for o in range(1, p.side):
            copy = remote(self.g2b, self.g1.at[own], self.ssem.at[3, o], self.rsem.at[3, o], p.at_x(o))
            self.sent.start(None, copy)
            other = self.rows16((p.x + p.side - o) % p.side, self.xq)
            self.waits.append(remote(self.g2b, self.g1.at[other], self.ssem.at[3, o], self.rsem.at[3, o], p.at_x(o)))
        self.g1[own, :] = self.g2b[...]

    def cg_start(self):
        self._wait()
        p = self.p
        own = self.rows16(p.k, self.half)
        other = self.rows16(1 - p.k, self.half)
        self.sent.start(None, remote(self.g1, self.fin.at[own], self.csend.at[1], self.crecv.at[1], p.at_core()))
        self.waits.append(remote(self.g1, self.fin.at[other], self.csend.at[1], self.crecv.at[1], p.at_core()))
        self.fin[own, :] = self.g1[...]

    def done(self):
        self._wait()

    def finish_sends(self):
        def body(o, _):
            z = (self.p.z + o) % self.p.depth

            @pl.when(z < self.owners)
            def _():
                self._z_out(o)[1].wait_send()

            @pl.when(self.p.z < self.owners)
            def _():
                self._z_back(o).wait_send()

            return 0

        lax.fori_loop(1, self.p.depth, body, 0)


def kernel(rows, cols, *refs):
    (contact, cotangent, conv_w, proj_w, out_map, out_conv, out_proj,
     own, grad, wf, wb, pw, hid, hslope, mid, slope, sh, wide, left, right, pack, mir, flat, acc, accp,
     hsend, hrecv, msend, mrecv, mloc, loc) = refs[:31]
    p = Place(rows, cols)
    sent = Sent()
    per = (len(refs) - 31) // len(GROUPS)
    reduces = []
    for index, blocks in enumerate(GROUPS):
        start = 31 + index * per
        reduces.append(Reduce(len(blocks) * BLOCK_ROWS, p, sent, refs[start : start + per]))

    barrier = pltpu.get_barrier_semaphore()

    def greet(device):
        pl.semaphore_signal(barrier, inc=1, device_id=device, device_id_type=MESH)

    count = jnp.int32(1 + 2 * (p.side - 1) + p.depth - 1)
    greet(p.at_core())
    for o in range(1, p.side):
        greet(p.at_x(o))
        greet(p.at_y(o))

    def greet_z(o, _):
        greet(p.at_z((p.z + o) % p.depth))
        return 0

    lax.fori_loop(1, p.depth, greet_z, 0)
    for dr, dc in MOVES:
        there = p.inside(dr, dc)
        pl.when(there)(functools.partial(greet, (p.r + dr, p.c + dc)))
        count = count + there.astype(jnp.int32)
    apart = p.q != p.r
    for h in range(2):
        pl.when(apart)(functools.partial(greet, (p.q, 2 * p.r + h)))
        count = count + apart.astype(jnp.int32)

    loads = [
        pltpu.make_async_copy(contact, own, loc.at[0]),
        pltpu.make_async_copy(cotangent, grad, loc.at[1]),
        pltpu.make_async_copy(conv_w, wf, loc.at[2]),
        pltpu.make_async_copy(proj_w, pw, loc.at[3]),
    ]
    for load in loads:
        load.start()
    pl.semaphore_wait(barrier, count)

    half = CELLS // 2

    def mirror_copies(turn, source, h):
        stays = (p.q == p.r) & (p.k == h)
        src = source.at[pl.ds(h * half, half)]
        dst = mir.at[turn, p.k]
        there = remote(src, dst, msend.at[turn, h], mrecv.at[turn, p.k], (p.q, 2 * p.r + h))
        here = pltpu.make_async_copy(src, dst, mloc.at[turn])
        return stays, there, here

    def mirror_start(turn, source, h):
        stays, there, here = mirror_copies(turn, source, h)
        sent.start(jnp.logical_not(stays), there)
        pl.when(stays)(here.start)

    def mirror_wait(turn, source):
        for h in range(2):
            stays = (p.q == p.r) & (p.k == h)
            dst = mir.at[turn, h]
            src = source.at[pl.ds(0, half)]
            there = remote(src, dst, msend.at[turn, h], mrecv.at[turn, h], (p.q, 2 * p.r + h))
            here = pltpu.make_async_copy(src, dst, mloc.at[turn])
            pl.when(jnp.logical_not(stays))(there.wait_recv)
            pl.when(stays)(here.wait)

    def mirror_spread(turn):
        def body(i, _):
            flat[pl.ds(pl.multiple_of(i * CHUNK, CHUNK), CHUNK), :] = mir[
                turn, i // 4, pl.ds(pl.multiple_of((i % 4) * CHUNK, CHUNK), CHUNK), :
            ].astype(F32)
            return 0

        lax.fori_loop(0, CELLS // CHUNK, body, 0)

    def mirror_rows(chunk):
        base = (chunk // (COLS // STEP)) * half + (chunk % (COLS // STEP)) * STEP
        return jnp.concatenate([flat[pl.ds(base + j, COLS, stride=COLS), :] for j in range(STEP)], axis=0)

    for h in range(2):
        mirror_start(0, contact, h)

    zero = functools.partial(jnp.zeros, dtype=BF)
    corner = MARGIN * MARGIN
    low, side_rows = (MARGIN + ROWS) * MARGIN, ROWS * MARGIN

    def fill(dr, dc, ref, start, size):
        @pl.when(jnp.logical_not(p.inside(dr, dc)))
        def _():
            def body(e, _):
                if ref is sh:
                    sh[e, 1, pl.ds(start, size), :] = zero((size, CH))
                else:
                    ref[e, pl.ds(start, size), :] = zero((size, CH))
                return 0

            lax.fori_loop(0, 2 * BLOCKS, body, 0)

    fill(-1, 0, sh, 0, MARGIN * COLS)
    fill(1, 0, sh, (MARGIN + ROWS) * COLS, MARGIN * COLS)
    for dc, ref in ((-1, left), (1, right)):
        fill(-1, dc, ref, 0, corner)
        fill(0, dc, ref, corner, side_rows)
        fill(1, dc, ref, low, corner)

    loads[2].wait()
    loads[3].wait()

    def flip(index, _):
        block, tap = index // TAPS, index % TAPS
        tile = wf[block, pl.ds(pl.multiple_of(tap * CH, CH), CH), :].astype(F32)
        wb[block, pl.ds(pl.multiple_of((TAPS - 1 - tap) * CH, CH), CH), :] = tile.T.astype(BF)
        return 0

    lax.fori_loop(0, BLOCKS * TAPS, flip, 0)
    loads[0].wait()
    loads[1].wait()

    def cells(chunk):
        return pl.ds(pl.multiple_of(chunk * CHUNK, CHUNK), CHUNK)

    def put_center(e, chunk, values):
        rounded = values.astype(BF)
        sh[e, 1, pl.ds(pl.multiple_of(chunk * CHUNK + MARGIN * COLS, CHUNK), CHUNK), :] = rounded
        cube = values.reshape(STEP, COLS, CH)
        wide[pl.ds(chunk * STEP + MARGIN, STEP), MARGIN : MARGIN + COLS, :] = cube
        edge = STEP * MARGIN
        at = pl.ds(pl.multiple_of(chunk * edge, edge), edge)
        pack[e, 0, at, :] = cube[:, :MARGIN, :].reshape(edge, CH).astype(BF)
        pack[e, 1, at, :] = cube[:, COLS - MARGIN :, :].reshape(edge, CH).astype(BF)

    def halo_copy(e, d, index):
        dr, dc = MOVES[index]
        strip = d * COLS
        if dr == 0:
            src, dst = pack.at[e, (dc + 1) // 2], (right if dc < 0 else left).at[e, pl.ds(corner, side_rows)]
        elif dc == 0:
            start, end = (MARGIN, MARGIN + ROWS) if dr < 0 else (MARGIN + ROWS - d, MARGIN - d)
            src = sh.at[e, 1, pl.ds(start * COLS, strip)]
            dst = sh.at[e, 1, pl.ds(end * COLS, strip)]
        else:
            src = pack.at[e, (dc + 1) // 2, pl.ds(0 if dr < 0 else side_rows - corner, corner)]
            dst = (right if dc < 0 else left).at[e, pl.ds(low if dr < 0 else 0, corner)]
        return remote(src, dst, hsend.at[e, index], hrecv.at[e, index], (p.r + dr, p.c + dc))

    def halo_start(e, d):
        for index, (dr, dc) in enumerate(MOVES):
            sent.start(p.inside(dr, dc), halo_copy(e, d, index))

    def halo_wait(e, d):
        for index, (dr, dc) in enumerate(MOVES):
            pl.when(p.inside(-dr, -dc))(halo_copy(e, d, index).wait_recv)

    def halo_build(e, d):
        def sides(i, _):
            at = pl.ds(pl.multiple_of(i * corner, corner), corner)
            to = pl.ds(i * MARGIN, MARGIN)
            wide[to, :MARGIN, :] = left[e, at, :].astype(F32).reshape(MARGIN, MARGIN, CH)
            wide[to, MARGIN + COLS :, :] = right[e, at, :].astype(F32).reshape(MARGIN, MARGIN, CH)
            return 0

        lax.fori_loop(0, HIGH // MARGIN, sides, 0)
        for start in (MARGIN - d, MARGIN + ROWS):
            strip = sh[e, 1, start * COLS : (start + d) * COLS, :].astype(F32)
            wide[start : start + d, MARGIN : MARGIN + COLS, :] = strip.reshape(d, COLS, CH)

        def shift(i, _):
            first = MARGIN - d + 4 * i
            for b in (0, 2):
                begin = MARGIN + (b - 1) * d
                cube = wide[pl.ds(first, 4), begin : begin + COLS, :]
                sh[e, b, pl.ds(pl.multiple_of(first * COLS, 2 * COLS), 4 * COLS), :] = cube.reshape(4 * COLS, CH).astype(BF)
            return 0

        lax.fori_loop(0, (ROWS + 2 * d) // 4, shift, 0)

    def windows(e, d, chunk):
        taps = []
        for a in range(3):
            start = pl.multiple_of(chunk * CHUNK + (MARGIN + (a - 1) * d) * COLS, 2 * COLS)
            for b in range(3):
                taps.append(sh[e, b, pl.ds(start, CHUNK), :])
        return jnp.concatenate(taps, axis=1)

    def each_chunk(body):
        def run(chunk, _):
            body(chunk)
            return 0

        lax.fori_loop(0, CHUNKS, run, 0)

    mirror_wait(0, contact)
    mirror_spread(0)

    def first(chunk):
        at = cells(chunk)
        hidden = (0.5 * (own[at, :].astype(F32) + mirror_rows(chunk))).astype(BF)
        hid[0, at, :] = hidden
        act, steep = gelu_parts(hidden.astype(F32))
        hslope[0, at, :] = steep
        put_center(0, chunk, act)

    each_chunk(first)

    for k in range(BLOCKS):
        d = 2 ** (k + 1)
        halo_start(k, d)
        halo_wait(k, d)
        halo_build(k, d)

        def forward(chunk, k=k, d=d):
            at = cells(chunk)
            middle, steep = gelu_parts(dot(windows(k, d, chunk), wf[k]))
            middle = middle.astype(BF)
            mid[k, at, :] = middle
            slope[k, at, :] = steep
            if k + 1 < BLOCKS:
                hidden = (hid[k, at, :].astype(F32) + dot(middle, pw[k])).astype(BF)
                hid[k + 1, at, :] = hidden
                act, bend = gelu_parts(hidden.astype(F32))
                hslope[k + 1, at, :] = bend
                put_center(k + 1, chunk, act)
            else:
                put_center(k + 1, chunk, dot_nt(grad[at, :], pw[k]) * steep)

        each_chunk(forward)

    queue = []

    def advance(steps):
        for _ in range(steps):
            if queue:
                queue.pop(0)()

    def phases(red):
        def both(a, b):
            def run():
                a()
                b()

            return run

        return [
            red.core_start,
            both(red.core_add, red.x_start),
            both(red.x_add, red.y_start),
            both(red.y_add, red.z_start),
            both(red.z_add, red.zg_start),
            both(red.zg_wait, red.yg_start),
            red.xg_start,
            red.cg_start,
            red.done,
        ]

    for k in reversed(range(BLOCKS)):
        d = 2 ** (k + 1)
        e = 2 * BLOCKS - 1 - k
        halo_start(e, d)
        advance(1)
        acc[...] = jnp.zeros_like(acc)
        accp[...] = jnp.zeros_like(accp)

        def weights(chunk, k=k, d=d, e=e):
            at = cells(chunk)
            back = sh[e, 1, pl.ds(pl.multiple_of(chunk * CHUNK + MARGIN * COLS, CHUNK), CHUNK), :]
            acc[...] += dot_tn(back, windows(k, d, chunk))
            accp[...] += dot_tn(mid[k, at, :], grad[at, :])

        each_chunk(weights)
        group = next(i for i, blocks in enumerate(GROUPS) if k in blocks)
        base = GROUPS[group].index(k) * BLOCK_ROWS
        red = reduces[group]
        for tap in range(TAPS):
            red.src[base + tap * CH : base + (tap + 1) * CH, :] = acc[:, tap * CH : (tap + 1) * CH].T.astype(BF)
        red.src[base + TAPS * CH : base + BLOCK_ROWS, :] = accp[...].astype(BF)
        if k == GROUPS[group][-1]:
            queue.extend(phases(red))
        advance(1)
        halo_wait(e, d)
        halo_build(e, d)
        advance(1)

        def backward(chunk, k=k, d=d, e=e):
            at = cells(chunk)
            change = dot(windows(e, d, chunk), wb[k]) * hslope[k, at, :]
            new = (grad[at, :].astype(F32) + change).astype(BF)
            grad[at, :] = new
            if k > 0:
                put_center(e + 1, chunk, dot_nt(new, pw[k - 1]) * slope[k - 1, at, :])

        each_chunk(backward)

    for h in range(2):
        mirror_start(1, grad, h)
    while queue:
        advance(1)
    scale = 1.0 / (rows * ROWS)
    for group, blocks in enumerate(GROUPS):
        for place, k in enumerate(blocks):
            base = place * BLOCK_ROWS
            fin = reduces[group].fin
            out_conv[k, :, :] = fin[base : base + TAPS * CH, :].astype(F32) * scale
            out_proj[k, :, :] = fin[base + TAPS * CH : base + BLOCK_ROWS, :].astype(F32) * scale
    mirror_wait(1, grad)
    mirror_spread(1)

    def last(chunk):
        at = cells(chunk)
        out_map[at, :] = (0.5 * (grad[at, :].astype(F32) + mirror_rows(chunk))).astype(BF)

    each_chunk(last)
    sent.finish()
    for red in reduces:
        red.finish_sends()


def solution(mesh):
    rows, cols = mesh.shape["row"], mesh.shape["col"]
    side = 4 if rows >= 16 else 2
    depth = (rows // side) * (cols // (2 * side))
    vmem, dma = pltpu.VMEM, pltpu.SemaphoreType.DMA
    scratch = [
        vmem((CELLS, CH), BF),
        vmem((CELLS, CH), BF),
        vmem((BLOCKS, TAPS * CH, CH), BF),
        vmem((BLOCKS, TAPS * CH, CH), BF),
        vmem((BLOCKS, CH, CH), BF),
        vmem((BLOCKS, CELLS, CH), BF),
        vmem((BLOCKS, CELLS, CH), F32),
        vmem((BLOCKS, CELLS, CH), BF),
        vmem((BLOCKS, CELLS, CH), F32),
        vmem((2 * BLOCKS, 3, HIGH * COLS, CH), BF),
        vmem((HIGH, WIDE, CH), F32),
        vmem((2 * BLOCKS, HIGH * MARGIN, CH), BF),
        vmem((2 * BLOCKS, HIGH * MARGIN, CH), BF),
        vmem((2 * BLOCKS, 2, ROWS * MARGIN, CH), BF),
        vmem((2, 2, CELLS // 2, CH), BF),
        vmem((CELLS, CH), F32),
        vmem((CH, TAPS * CH), F32),
        vmem((CH, CH), F32),
        dma((2 * BLOCKS, 8)),
        dma((2 * BLOCKS, 8)),
        dma((2, 2)),
        dma((2, 2)),
        dma((2,)),
        dma((4,)),
    ]
    for blocks in GROUPS:
        scratch += Reduce.scratch(len(blocks) * BLOCK_ROWS, side, depth)

    def body(contact_map, cotangent, conv_weight, proj_weight):
        out_map, out_conv, out_proj = pl.pallas_call(
            functools.partial(kernel, rows, cols),
            out_shape=(
                jax.ShapeDtypeStruct((CELLS, CH), BF),
                jax.ShapeDtypeStruct((BLOCKS, TAPS * CH, CH), F32),
                jax.ShapeDtypeStruct((BLOCKS, CH, CH), F32),
            ),
            in_specs=[pl.BlockSpec(memory_space=pl.ANY)] * 4,
            out_specs=(pl.BlockSpec(memory_space=pltpu.VMEM),) * 3,
            scratch_shapes=scratch,
            compiler_params=pltpu.CompilerParams(
                collective_id=0, has_side_effects=True, vmem_limit_bytes=56 * 1024 * 1024
            ),
        )(
            contact_map.reshape(CELLS, CH),
            cotangent.reshape(CELLS, CH),
            conv_weight.reshape(BLOCKS, TAPS * CH, CH),
            proj_weight,
        )
        return (
            out_map.reshape(ROWS, COLS, CH),
            out_conv.reshape(BLOCKS, 3, 3, CH, CH),
            out_proj,
        )

    in_specs = (P("row", "col", None), P("row", "col", None), P(), P())
    out_specs = (P("row", "col", None), P(), P())
    return jax.shard_map(body, mesh=mesh, in_specs=in_specs, out_specs=out_specs, check_vma=False)
```

```python
import functools

import jax
import jax.numpy as jnp
from jax import lax
from jax.experimental import pallas as pl
from jax.experimental.pallas import tpu as pltpu
from jax.sharding import PartitionSpec as P

MESH = pl.DeviceIdType.MESH
BF = jnp.bfloat16
F32 = jnp.float32
ROWS, COLS, CH, MARGIN = 64, 32, 128, 8
CELLS = ROWS * COLS
CORNER = 16
TALL = ROWS + 2 * CORNER
HIGH, WIDE = ROWS + 2 * MARGIN, COLS + 2 * MARGIN
STEP = 32
CHUNK = STEP * COLS
CHUNKS = ROWS // STEP
TAPS = 9
BLOCKS = 3
SLOPE_C = 0.7978845608028654
CUBIC = 0.044715
MOVES = ((0, -1), (0, 1), (-1, 0), (1, 0), (-1, -1), (-1, 1), (1, -1), (1, 1))
GROUPS = ((2, 1, 0),)
BLOCK_ROWS = (TAPS + 1) * CH
PIECES = 4
EARLY = 4
CONV_ROWS = BLOCKS * TAPS * CH


def gelu_parts(v):
    u = v * v
    t = jnp.tanh(SLOPE_C * v * (1.0 + CUBIC * u))
    half = 0.5 + 0.5 * t
    slope = half + (0.5 * SLOPE_C) * v * (1.0 - t * t) * (1.0 + 3.0 * CUBIC * u)
    return v * half, slope


def dot(a, b):
    return jnp.dot(a, b, preferred_element_type=F32)


def dot_nt(a, b):
    return lax.dot_general(a, b, (((1,), (1,)), ((), ())), preferred_element_type=F32)


def dot_tn(a, b):
    return lax.dot_general(a, b, (((0,), (0,)), ((), ())), preferred_element_type=F32)


class Place:
    def __init__(self, rows, cols):
        self.rows, self.cols = rows, cols
        self.side = 4 if rows >= 16 else 2
        self.depth = (rows // self.side) * (cols // (2 * self.side))
        self.parts = rows // self.side
        self.r, self.c = lax.axis_index("row"), lax.axis_index("col")
        self.y, self.zl = self.r % self.side, self.r // self.side
        self.k = self.c % 2
        self.q = self.c // 2
        self.x, self.zh = self.q % self.side, self.q // self.side
        self.z = self.zh * self.parts + self.zl

    def at_core(self):
        return (self.r, self.c + 1 - 2 * self.k)

    def at_x(self, offset):
        x = (self.x + offset) % self.side
        return (self.r, self.zh * 2 * self.side + 2 * x + self.k)

    def at_y(self, offset):
        y = (self.y + offset) % self.side
        return (self.zl * self.side + y, self.c)

    def at_z(self, z):
        zh, zl = z // self.parts, z % self.parts
        return (zl * self.side + self.y, zh * 2 * self.side + 2 * self.x + self.k)

    def inside(self, dr, dc):
        r, c = self.r + dr, self.c + dc
        return (r >= 0) & (r < self.rows) & (c >= 0) & (c < self.cols)


class Sent:
    def __init__(self):
        self.items = []

    def start(self, cond, copy):
        if cond is None:
            copy.start()
        else:
            pl.when(cond)(copy.start)
        self.items.append((cond, copy))

    def finish(self):
        for cond, copy in self.items:
            if cond is None:
                copy.wait_send()
            else:
                pl.when(cond)(copy.wait_send)


def remote(src, dst, send, recv, device):
    return pltpu.make_async_remote_copy(
        src_ref=src, dst_ref=dst, send_sem=send, recv_sem=recv, device_id=device, device_id_type=MESH
    )


class Reduce:
    @staticmethod
    def sizes(n, side, depth):
        half = n // 2
        xq = half // side
        yq = xq // side
        tiles = yq // 8
        zr = 8 * -(-tiles // depth)
        return half, xq, yq, zr

    @staticmethod
    def scratch(n, side, depth):
        half, xq, yq, zr = Reduce.sizes(n, side, depth)
        dma = pltpu.SemaphoreType.DMA
        return [
            pltpu.VMEM((n, CH), BF),
            pltpu.VMEM((half, CH), BF),
            pltpu.VMEM((half, CH), BF),
            pltpu.VMEM((side - 1, xq, CH), BF),
            pltpu.VMEM((xq, CH), F32),
            pltpu.VMEM((side - 1, yq, CH), F32),
            pltpu.VMEM((yq, CH), F32),
            pltpu.VMEM((depth, zr, CH), F32),
            pltpu.VMEM((yq, CH), F32),
            pltpu.VMEM((xq, CH), F32),
            pltpu.VMEM((xq, CH), BF),
            pltpu.VMEM((half, CH), BF),
            pltpu.VMEM((n, CH), BF),
            dma((4, 4)),
            dma((4, 4)),
            dma((4,)),
            dma((4,)),
            dma((2, depth)),
            dma((2, depth)),
        ]

    def __init__(self, n, place, sent, refs):
        self.n, self.p, self.sent = n, place, sent
        self.half, self.xq, self.yq, self.zr = Reduce.sizes(n, place.side, place.depth)
        self.owners = self.yq // self.zr
        (self.src, self.rc, self.s1, self.rx, self.s2, self.ry, self.s3, self.rz, self.g3, self.g2,
         self.g2b, self.g1, self.fin, self.ssem, self.rsem, self.csend, self.crecv, self.zsend,
         self.zrecv) = refs
        self.waits = []

    def rows(self, index, size):
        return pl.ds(pl.multiple_of(index * size, 8), size)

    def rows16(self, index, size):
        return pl.ds(pl.multiple_of(index * size, 16), size)

    def _wait(self):
        for copy in self.waits:
            copy.wait_recv()
        self.waits = []

    def _send(self, src, dst, send, recv, device):
        copy = remote(src, dst, send, recv, device)
        self.sent.start(None, copy)
        self.waits.append(copy)

    def core_start(self):
        p = self.p
        self._send(self.src.at[self.rows16(1 - p.k, self.half)], self.rc, self.csend.at[0], self.crecv.at[0], p.at_core())

    def core_add(self):
        self._wait()
        own = self.rows16(self.p.k, self.half)
        self.s1[...] = (self.src[own, :].astype(F32) + self.rc[...].astype(F32)).astype(BF)

    def x_start(self):
        p = self.p
        for o in range(1, p.side):
            other = (p.x + o) % p.side
            self._send(self.s1.at[self.rows16(other, self.xq)], self.rx.at[o - 1], self.ssem.at[0, o], self.rsem.at[0, o], p.at_x(o))

    def x_add(self):
        self._wait()
        total = self.s1[self.rows16(self.p.x, self.xq), :].astype(F32)
        for o in range(1, self.p.side):
            total = total + self.rx[o - 1].astype(F32)
        self.s2[...] = total

    def y_start(self):
        p = self.p
        for o in range(1, p.side):
            other = (p.y + o) % p.side
            self._send(self.s2.at[self.rows(other, self.yq)], self.ry.at[o - 1], self.ssem.at[1, o], self.rsem.at[1, o], p.at_y(o))

    def y_add(self):
        self._wait()
        total = self.s2[self.rows(self.p.y, self.yq), :]
        for o in range(1, self.p.side):
            total = total + self.ry[o - 1]
        self.s3[...] = total

    def _z_out(self, o):
        p = self.p
        z = (p.z + o) % p.depth
        return z, remote(self.s3.at[self.rows(z, self.zr)], self.rz.at[o], self.zsend.at[0, o], self.zrecv.at[0, o], p.at_z(z))

    def z_start(self):
        def body(o, _):
            z = (self.p.z + o) % self.p.depth

            @pl.when(z < self.owners)
            def _():
                self._z_out(o)[1].start()

            return 0

        lax.fori_loop(1, self.p.depth, body, 0)

    def z_add(self):
        p = self.p

        @pl.when(p.z < self.owners)
        def _():
            def wait(o, _):
                remote(self.rz.at[o], self.rz.at[o], self.zsend.at[0, o], self.zrecv.at[0, o], p.at_z(p.z)).wait_recv()
                return 0

            lax.fori_loop(1, p.depth, wait, 0)
            own = self.rows(p.z, self.zr)
            total = self.s3[own, :]
            for o in range(1, p.depth):
                total = total + self.rz[o]
            self.g3[own, :] = total

    def _z_back(self, o):
        p = self.p
        z = (p.z + o) % p.depth
        own = self.g3.at[self.rows(p.z, self.zr)]
        return remote(own, own, self.zsend.at[1, o], self.zrecv.at[1, p.z], p.at_z(z))

    def zg_start(self):
        p = self.p

        @pl.when(p.z < self.owners)
        def _():
            def body(o, _):
                self._z_back(o).start()
                return 0

            lax.fori_loop(1, p.depth, body, 0)

    def zg_wait(self):
        p = self.p

        def body(z, _):
            @pl.when(z != p.z)
            def _():
                part = self.g3.at[self.rows(z, self.zr)]
                remote(part, part, self.zsend.at[1, z], self.zrecv.at[1, z], p.at_z(z)).wait_recv()

            return 0

        lax.fori_loop(0, self.owners, body, 0)

    def yg_start(self):
        p = self.p
        own = self.rows(p.y, self.yq)
        for o in range(1, p.side):
            copy = remote(self.g3, self.g2.at[own], self.ssem.at[2, o], self.rsem.at[2, o], p.at_y(o))
            self.sent.start(None, copy)
            other = self.rows((p.y + p.side - o) % p.side, self.yq)
            self.waits.append(remote(self.g3, self.g2.at[other], self.ssem.at[2, o], self.rsem.at[2, o], p.at_y(o)))
        self.g2[own, :] = self.g3[...]

    def xg_start(self):
        self._wait()
        p = self.p
        self.g2b[...] = self.g2[...].astype(BF)
        own = self.rows16(p.x, self.xq)
        for o in range(1, p.side):
            copy = remote(self.g2b, self.g1.at[own], self.ssem.at[3, o], self.rsem.at[3, o], p.at_x(o))
            self.sent.start(None, copy)
            other = self.rows16((p.x + p.side - o) % p.side, self.xq)
            self.waits.append(remote(self.g2b, self.g1.at[other], self.ssem.at[3, o], self.rsem.at[3, o], p.at_x(o)))
        self.g1[own, :] = self.g2b[...]

    def cg_start(self):
        self._wait()
        p = self.p
        own = self.rows16(p.k, self.half)
        other = self.rows16(1 - p.k, self.half)
        self.sent.start(None, remote(self.g1, self.fin.at[own], self.csend.at[1], self.crecv.at[1], p.at_core()))
        self.waits.append(remote(self.g1, self.fin.at[other], self.csend.at[1], self.crecv.at[1], p.at_core()))
        self.fin[own, :] = self.g1[...]

    def done(self):
        self._wait()

    def finish_sends(self):
        def body(o, _):
            z = (self.p.z + o) % self.p.depth

            @pl.when(z < self.owners)
            def _():
                self._z_out(o)[1].wait_send()

            @pl.when(self.p.z < self.owners)
            def _():
                self._z_back(o).wait_send()

            return 0

        lax.fori_loop(1, self.p.depth, body, 0)


def kernel(rows, cols, *refs):
    (contact, cotangent, conv_w, proj_w, out_map, out_sum,
     own, grad, wf, wb, pw, hid, hslope, mid, slope, sh, wide, rim, left, right, pack, mir, flat, acc, accp,
     hsend, hrecv, passing, msend, mrecv, psend, precv, mloc, loc) = refs[:34]
    p = Place(rows, cols)
    sent = Sent()
    per = (len(refs) - 34) // len(GROUPS)
    reduces = []
    for index, blocks in enumerate(GROUPS):
        start = 34 + index * per
        reduces.append(Reduce(len(blocks) * BLOCK_ROWS, p, sent, refs[start : start + per]))

    barrier = pltpu.get_barrier_semaphore()

    def greet(device):
        pl.semaphore_signal(barrier, inc=1, device_id=device, device_id_type=MESH)

    count = jnp.int32(1 + 2 * (p.side - 1) + p.depth - 1)
    greet(p.at_core())
    for o in range(1, p.side):
        greet(p.at_x(o))
        greet(p.at_y(o))

    def greet_z(o, _):
        greet(p.at_z((p.z + o) % p.depth))
        return 0

    lax.fori_loop(1, p.depth, greet_z, 0)
    for dr, dc in MOVES:
        there = p.inside(dr, dc)
        pl.when(there)(functools.partial(greet, (p.r + dr, p.c + dc)))
        count = count + there.astype(jnp.int32)
    apart, turned, swapped = p.q != p.r, p.x != p.y, p.zh != p.zl
    for h in range(2):
        pl.when(apart)(functools.partial(greet, (p.q, 2 * p.r + h)))
        pl.when(swapped)(functools.partial(greet, (p.zh * p.side + p.y, p.zl * 2 * p.side + 2 * p.x + h)))
        count = count + apart.astype(jnp.int32) + swapped.astype(jnp.int32)
    pl.when(turned)(functools.partial(greet, (p.zl * p.side + p.x, p.zh * 2 * p.side + 2 * p.y + p.k)))
    count = count + turned.astype(jnp.int32)

    loads = [
        pltpu.make_async_copy(contact, own, loc.at[0]),
        pltpu.make_async_copy(cotangent, grad, loc.at[1]),
        pltpu.make_async_copy(conv_w, wf, loc.at[2]),
        pltpu.make_async_copy(proj_w, pw, loc.at[3]),
    ]
    for load in loads:
        load.start()
    pl.semaphore_wait(barrier, count)

    half = CELLS // 2
    piece = half // PIECES
    by_relay = (p.x != p.y) & (p.zh != p.zl)
    mirrored = (p.q, 2 * p.r)
    relay = (p.zl * p.side + p.x, p.zh * 2 * p.side + 2 * p.y + p.k)
    beyond = (p.zh * p.side + p.y, p.zl * 2 * p.side + 2 * p.x)
    every = [(h, n) for n in range(PIECES) for h in range(2)]
    odd = [(h, n) for h, n in every if n % 2 == 1]

    def part_of(n):
        return pl.ds(n * piece, piece)

    def direct(turn, source, h, n):
        src = source.at[pl.ds(h * half + n * piece, piece)]
        dst = mir.at[turn, p.k, part_of(n)]
        device = (mirrored[0], mirrored[1] + h)
        return remote(src, dst, msend.at[turn, h, n], mrecv.at[turn, p.k, n], device)

    def staying(turn, source, n):
        src = source.at[pl.ds(p.k * half + n * piece, piece)]
        return pltpu.make_async_copy(src, mir.at[turn, p.k, part_of(n)], mloc.at[turn, n])

    def to_relay(turn, source, h, n):
        src = source.at[pl.ds(h * half + n * piece, piece)]
        return remote(src, passing.at[turn, h, part_of(n)], msend.at[turn, h, n], precv.at[turn, h, n], relay)

    def from_relay(turn, h, n):
        dst = mir.at[turn, p.k, part_of(n)]
        device = (beyond[0], beyond[1] + h)
        return remote(passing.at[turn, h, part_of(n)], dst, psend.at[turn, h, n], mrecv.at[turn, p.k, n], device)

    same = p.q == p.r

    def mirror_first(turn, source):
        for h, n in odd:
            sent.start(by_relay, to_relay(turn, source, h, n))

    def mirror_direct(turn, source, pieces):
        for h, n in pieces:
            stays = same & (p.k == h)
            goes = jnp.logical_not(stays)
            if n % 2 == 1:
                goes = goes & jnp.logical_not(by_relay)
            sent.start(goes, direct(turn, source, h, n))
            pl.when(stays)(staying(turn, source, n).start)

    def mirror_forward(turn, source):
        for h, n in odd:
            pl.when(by_relay)(to_relay(turn, source, h, n).wait_recv)
            sent.start(by_relay, from_relay(turn, h, n))

    def mirror_wait(turn, source):
        for h, n in every:
            stays = same & (p.k == h)
            arrives = remote(mir.at[turn, h, part_of(n)], mir.at[turn, h, part_of(n)], msend.at[turn, h, n],
                             mrecv.at[turn, h, n], (mirrored[0], mirrored[1] + h))
            pl.when(jnp.logical_not(stays))(arrives.wait_recv)
            pl.when(stays)(staying(turn, source, n).wait)

    def mirror_spread(turn):
        steps = half // CHUNK

        def body(i, _):
            flat[pl.ds(pl.multiple_of(i * CHUNK, CHUNK), CHUNK), :] = mir[
                turn, i // steps, pl.ds(pl.multiple_of((i % steps) * CHUNK, CHUNK), CHUNK), :
            ].astype(F32)
            return 0

        lax.fori_loop(0, CELLS // CHUNK, body, 0)

    def mirror_rows(chunk):
        base = (chunk // (COLS // STEP)) * half + (chunk % (COLS // STEP)) * STEP
        return jnp.concatenate([flat[pl.ds(base + j, COLS, stride=COLS), :] for j in range(STEP)], axis=0)

    mirror_first(0, contact)
    mirror_direct(0, contact, every)
    mirror_forward(0, contact)

    zero = functools.partial(jnp.zeros, dtype=BF)

    def fill(dr, dc, ref, at, shape):
        @pl.when(jnp.logical_not(p.inside(dr, dc)))
        def _():
            def body(e, _):
                ref[(e, *at)] = zero(shape)
                return 0

            lax.fori_loop(0, 2 * BLOCKS, body, 0)

    strip = MARGIN * COLS
    fill(-1, 0, sh, (1, pl.ds(0, strip)), (strip, CH))
    fill(1, 0, sh, (1, pl.ds((MARGIN + ROWS) * COLS, strip)), (strip, CH))
    for dc, ref in ((-1, left), (1, right)):
        fill(-1, dc, ref, (slice(None), pl.ds(0, CORNER)), (MARGIN, CORNER, CH))
        fill(0, dc, ref, (slice(None), pl.ds(CORNER, ROWS)), (MARGIN, ROWS, CH))
        fill(1, dc, ref, (slice(None), pl.ds(CORNER + ROWS, CORNER)), (MARGIN, CORNER, CH))

    loads[2].wait()
    loads[3].wait()

    def flip(index, _):
        block, tap = index // TAPS, index % TAPS
        tile = wf[block, pl.ds(pl.multiple_of(tap * CH, CH), CH), :].astype(F32)
        wb[block, pl.ds(pl.multiple_of((TAPS - 1 - tap) * CH, CH), CH), :] = tile.T.astype(BF)
        return 0

    lax.fori_loop(0, BLOCKS * TAPS, flip, 0)
    loads[0].wait()
    loads[1].wait()

    def cells(chunk):
        return pl.ds(pl.multiple_of(chunk * CHUNK, CHUNK), CHUNK)

    def put_center(e, chunk, values):
        rounded = values.astype(BF)
        sh[e, 1, pl.ds(pl.multiple_of(chunk * CHUNK + MARGIN * COLS, MARGIN * COLS), CHUNK), :] = rounded
        cube = values.reshape(STEP, COLS, CH)
        wide[pl.ds(chunk * STEP + MARGIN, STEP), MARGIN : MARGIN + COLS, :] = cube
        edge = STEP * MARGIN
        at = pl.ds(pl.multiple_of(chunk * edge, edge), edge)
        rim[0, at, :] = cube[:, :MARGIN, :].reshape(edge, CH)
        rim[1, at, :] = cube[:, COLS - MARGIN :, :].reshape(edge, CH)

    def halo_copy(e, d, index):
        dr, dc = MOVES[index]
        strip = d * COLS
        side = (dc + 1) // 2
        margin = right if dc < 0 else left
        if dr == 0:
            src = pack.at[e, side, pl.ds(0, d)]
            dst = margin.at[e, pl.ds(0, d), pl.ds(CORNER, ROWS)]
        elif dc == 0:
            start, end = (MARGIN, MARGIN + ROWS) if dr < 0 else (MARGIN + ROWS - d, MARGIN - d)
            src = sh.at[e, 1, pl.ds(start * COLS, strip)]
            dst = sh.at[e, 1, pl.ds(end * COLS, strip)]
        else:
            src = pack.at[e, side, pl.ds(0, d), pl.ds(0 if dr < 0 else ROWS - CORNER, CORNER)]
            dst = margin.at[e, pl.ds(0, d), pl.ds(CORNER + ROWS if dr < 0 else 0, CORNER)]
        return remote(src, dst, hsend.at[e, index], hrecv.at[e, index], (p.r + dr, p.c + dc))

    def halo_start(e, d):
        for j in range(d):
            pack[e, 0, j, :, :] = rim[0, pl.ds(j, ROWS, stride=MARGIN), :].astype(BF)
            pack[e, 1, j, :, :] = rim[1, pl.ds(MARGIN - d + j, ROWS, stride=MARGIN), :].astype(BF)
        for index, (dr, dc) in enumerate(MOVES):
            sent.start(p.inside(dr, dc), halo_copy(e, d, index))

    def halo_wait(e, d):
        for index, (dr, dc) in enumerate(MOVES):
            pl.when(p.inside(-dr, -dc))(halo_copy(e, d, index).wait_recv)

    def halo_build(e, d):
        for j in range(d):
            inner = CORNER - MARGIN
            rim[0, pl.ds(MARGIN - d + j, HIGH, stride=MARGIN), :] = left[e, j, :, :].astype(F32)[inner : inner + HIGH]
            rim[1, pl.ds(j, HIGH, stride=MARGIN), :] = right[e, j, :, :].astype(F32)[inner : inner + HIGH]
        wide[:, :MARGIN, :] = rim[0].reshape(HIGH, MARGIN, CH)
        wide[:, MARGIN + COLS :, :] = rim[1].reshape(HIGH, MARGIN, CH)
        for start in (MARGIN - d, MARGIN + ROWS):
            edge = sh[e, 1, start * COLS : (start + d) * COLS, :].astype(F32)
            wide[start : start + d, MARGIN : MARGIN + COLS, :] = edge.reshape(d, COLS, CH)

        def shift(i, _):
            first = MARGIN - d + 4 * i
            for b in (0, 2):
                begin = MARGIN + (b - 1) * d
                moved = wide[pl.ds(first, 4), begin : begin + COLS, :]
                sh[e, b, pl.ds(pl.multiple_of(first * COLS, 2 * COLS), 4 * COLS), :] = moved.reshape(4 * COLS, CH).astype(BF)
            return 0

        lax.fori_loop(0, (ROWS + 2 * d) // 4, shift, 0)

    def windows(e, d, chunk):
        taps = []
        for a in range(3):
            start = pl.multiple_of(chunk * CHUNK + (MARGIN + (a - 1) * d) * COLS, 2 * COLS)
            for b in range(3):
                taps.append(sh[e, b, pl.ds(start, CHUNK), :])
        return jnp.concatenate(taps, axis=1)

    def each_chunk(body):
        def run(chunk, _):
            body(chunk)
            return 0

        lax.fori_loop(0, CHUNKS, run, 0)

    mirror_wait(0, contact)
    mirror_spread(0)

    def first(chunk):
        at = cells(chunk)
        hidden = (0.5 * (own[at, :].astype(F32) + mirror_rows(chunk))).astype(BF)
        hid[0, at, :] = hidden
        act, steep = gelu_parts(hidden.astype(F32))
        hslope[0, at, :] = steep
        put_center(0, chunk, act)

    each_chunk(first)

    for k in range(BLOCKS):
        d = 2 ** (k + 1)
        halo_start(k, d)
        halo_wait(k, d)
        halo_build(k, d)

        def forward(chunk, k=k, d=d):
            at = cells(chunk)
            middle, steep = gelu_parts(dot(windows(k, d, chunk), wf[k]))
            middle = middle.astype(BF)
            mid[k, at, :] = middle
            slope[k, at, :] = steep
            if k + 1 < BLOCKS:
                hidden = (hid[k, at, :].astype(F32) + dot(middle, pw[k])).astype(BF)
                hid[k + 1, at, :] = hidden
                act, bend = gelu_parts(hidden.astype(F32))
                hslope[k + 1, at, :] = bend
                put_center(k + 1, chunk, act)
            else:
                put_center(k + 1, chunk, dot_nt(grad[at, :], pw[k]) * steep)

        each_chunk(forward)

    queues = []

    def advance(steps):
        for queue in queues * steps:
            if queue:
                queue.pop(0)()

    def phases(red):
        def both(a, b):
            def run():
                a()
                b()

            return run

        return [
            red.core_start,
            both(red.core_add, red.x_start),
            both(red.x_add, red.y_start),
            both(red.y_add, red.z_start),
            both(red.z_add, red.zg_start),
            both(red.zg_wait, red.yg_start),
            red.xg_start,
            red.cg_start,
            red.done,
        ]

    for k in reversed(range(BLOCKS)):
        d = 2 ** (k + 1)
        e = 2 * BLOCKS - 1 - k
        halo_start(e, d)
        acc[...] = jnp.zeros_like(acc)
        accp[...] = jnp.zeros_like(accp)

        def weights(chunk, k=k, d=d, e=e):
            at = cells(chunk)
            back = sh[e, 1, pl.ds(pl.multiple_of(chunk * CHUNK + MARGIN * COLS, MARGIN * COLS), CHUNK), :]
            acc[...] += dot_tn(back, windows(k, d, chunk))
            accp[...] += dot_tn(mid[k, at, :], grad[at, :])

        each_chunk(weights)
        group = next(i for i, blocks in enumerate(GROUPS) if k in blocks)
        base = GROUPS[group].index(k) * BLOCK_ROWS
        red = reduces[group]
        for tap in range(TAPS):
            red.src[base + tap * CH : base + (tap + 1) * CH, :] = acc[:, tap * CH : (tap + 1) * CH].T.astype(BF)
        red.src[base + TAPS * CH : base + BLOCK_ROWS, :] = accp[...].astype(BF)
        if k == GROUPS[group][-1]:
            queues.append(phases(red))
        advance(1)
        halo_wait(e, d)
        halo_build(e, d)

        def backward(chunk, k=k, d=d, e=e):
            at = cells(chunk)
            change = dot(windows(e, d, chunk), wb[k]) * hslope[k, at, :]
            new = (grad[at, :].astype(F32) + change).astype(BF)
            grad[at, :] = new
            if k > 0:
                put_center(e + 1, chunk, dot_nt(new, pw[k - 1]) * slope[k - 1, at, :])

        each_chunk(backward)
        advance(1)

    mirror_first(1, grad)
    mirror_direct(1, grad, every[:EARLY])
    mirror_forward(1, grad)
    advance(1)
    mirror_direct(1, grad, every[EARLY:])
    while any(queues):
        advance(1)
    for group, blocks in enumerate(GROUPS):
        for place, k in enumerate(blocks):
            base = place * BLOCK_ROWS
            fin = reduces[group].fin
            out_sum[k * TAPS * CH : (k + 1) * TAPS * CH, :] = fin[base : base + TAPS * CH, :]
            out_sum[CONV_ROWS + k * CH : CONV_ROWS + (k + 1) * CH, :] = fin[base + TAPS * CH : base + BLOCK_ROWS, :]
    mirror_wait(1, grad)
    mirror_spread(1)

    def last(chunk):
        at = cells(chunk)
        out_map[at, :] = (0.5 * (grad[at, :].astype(F32) + mirror_rows(chunk))).astype(BF)

    each_chunk(last)
    sent.finish()
    for red in reduces:
        red.finish_sends()


def solution(mesh):
    rows, cols = mesh.shape["row"], mesh.shape["col"]
    side = 4 if rows >= 16 else 2
    depth = (rows // side) * (cols // (2 * side))
    vmem, dma = pltpu.VMEM, pltpu.SemaphoreType.DMA
    scratch = [
        vmem((CELLS, CH), BF),
        vmem((CELLS, CH), BF),
        vmem((BLOCKS, TAPS * CH, CH), BF),
        vmem((BLOCKS, TAPS * CH, CH), BF),
        vmem((BLOCKS, CH, CH), BF),
        vmem((BLOCKS, CELLS, CH), BF),
        vmem((BLOCKS, CELLS, CH), F32),
        vmem((BLOCKS, CELLS, CH), BF),
        vmem((BLOCKS, CELLS, CH), F32),
        vmem((2 * BLOCKS, 3, HIGH * COLS, CH), BF),
        vmem((HIGH, WIDE, CH), F32),
        vmem((2, HIGH * MARGIN, CH), F32),
        vmem((2 * BLOCKS, MARGIN, TALL, CH), BF),
        vmem((2 * BLOCKS, MARGIN, TALL, CH), BF),
        vmem((2 * BLOCKS, 2, MARGIN, ROWS, CH), BF),
        vmem((2, 2, CELLS // 2, CH), BF),
        vmem((CELLS, CH), F32),
        vmem((CH, TAPS * CH), F32),
        vmem((CH, CH), F32),
        dma((2 * BLOCKS, 8)),
        dma((2 * BLOCKS, 8)),
        vmem((2, 2, CELLS // 2, CH), BF),
        dma((2, 2, PIECES)),
        dma((2, 2, PIECES)),
        dma((2, 2, PIECES)),
        dma((2, 2, PIECES)),
        dma((2, PIECES)),
        dma((4,)),
    ]
    for blocks in GROUPS:
        scratch += Reduce.scratch(len(blocks) * BLOCK_ROWS, side, depth)

    scale = 1.0 / (rows * ROWS)

    def body(contact_map, cotangent, conv_weight, proj_weight):
        out_map, out_sum = pl.pallas_call(
            functools.partial(kernel, rows, cols),
            out_shape=(
                jax.ShapeDtypeStruct((CELLS, CH), BF),
                jax.ShapeDtypeStruct((BLOCKS * BLOCK_ROWS, CH), BF),
            ),
            in_specs=[pl.BlockSpec(memory_space=pl.ANY)] * 4,
            out_specs=(pl.BlockSpec(memory_space=pltpu.VMEM),) * 2,
            scratch_shapes=scratch,
            compiler_params=pltpu.CompilerParams(
                collective_id=0, has_side_effects=True, vmem_limit_bytes=56 * 1024 * 1024
            ),
        )(
            contact_map.reshape(CELLS, CH),
            cotangent.reshape(CELLS, CH),
            conv_weight.reshape(BLOCKS, TAPS * CH, CH),
            proj_weight,
        )
        return (
            out_map.reshape(ROWS, COLS, CH),
            (out_sum[:CONV_ROWS].astype(F32) * scale).reshape(BLOCKS, 3, 3, CH, CH),
            (out_sum[CONV_ROWS:].astype(F32) * scale).reshape(BLOCKS, CH, CH),
        )

    in_specs = (P("row", "col", None), P("row", "col", None), P(), P())
    out_specs = (P("row", "col", None), P(), P())
    return jax.shard_map(body, mesh=mesh, in_specs=in_specs, out_specs=out_specs, check_vma=False)
```

```python
import functools

import jax
import jax.numpy as jnp
from jax import lax
from jax.experimental import pallas as pl
from jax.experimental.pallas import tpu as pltpu
from jax.sharding import PartitionSpec as P

MESH = pl.DeviceIdType.MESH
BF = jnp.bfloat16
F32 = jnp.float32
ROWS, COLS, CH, MARGIN = 64, 32, 128, 8
CELLS = ROWS * COLS
CORNER = 16
TALL = ROWS + 2 * CORNER
HIGH, WIDE = ROWS + 2 * MARGIN, COLS + 2 * MARGIN
STEP = 32
CHUNK = STEP * COLS
CHUNKS = ROWS // STEP
TAPS = 9
BLOCKS = 3
SLOPE_C = 0.7978845608028654
CUBIC = 0.044715
MOVES = ((-1, -1), (-1, 1), (1, -1), (1, 1), (0, -1), (0, 1), (-1, 0), (1, 0))
GROUPS = ((2, 1, 0),)
BLOCK_ROWS = (TAPS + 1) * CH
PIECES = 4
EARLY = 4
CONV_ROWS = BLOCKS * TAPS * CH


def gelu_parts(v):
    u = v * v
    t = jnp.tanh(SLOPE_C * v * (1.0 + CUBIC * u))
    half = 0.5 + 0.5 * t
    slope = half + (0.5 * SLOPE_C) * v * (1.0 - t * t) * (1.0 + 3.0 * CUBIC * u)
    return v * half, slope


def dot(a, b):
    return jnp.dot(a, b, preferred_element_type=F32)


def dot_nt(a, b):
    return lax.dot_general(a, b, (((1,), (1,)), ((), ())), preferred_element_type=F32)


def dot_tn(a, b):
    return lax.dot_general(a, b, (((0,), (0,)), ((), ())), preferred_element_type=F32)


class Place:
    def __init__(self, rows, cols):
        self.rows, self.cols = rows, cols
        self.side = 4 if rows >= 16 else 2
        self.depth = (rows // self.side) * (cols // (2 * self.side))
        self.parts = rows // self.side
        self.r, self.c = lax.axis_index("row"), lax.axis_index("col")
        self.y, self.zl = self.r % self.side, self.r // self.side
        self.k = self.c % 2
        self.q = self.c // 2
        self.x, self.zh = self.q % self.side, self.q // self.side
        self.z = self.zh * self.parts + self.zl

    def at_core(self):
        return (self.r, self.c + 1 - 2 * self.k)

    def at_x(self, offset):
        x = (self.x + offset) % self.side
        return (self.r, self.zh * 2 * self.side + 2 * x + self.k)

    def at_y(self, offset):
        y = (self.y + offset) % self.side
        return (self.zl * self.side + y, self.c)

    def at_z(self, z):
        zh, zl = z // self.parts, z % self.parts
        return (zl * self.side + self.y, zh * 2 * self.side + 2 * self.x + self.k)

    def inside(self, dr, dc):
        r, c = self.r + dr, self.c + dc
        return (r >= 0) & (r < self.rows) & (c >= 0) & (c < self.cols)


class Sent:
    def __init__(self):
        self.items = []

    def start(self, cond, copy):
        if cond is None:
            copy.start()
        else:
            pl.when(cond)(copy.start)
        self.items.append((cond, copy))

    def finish(self):
        for cond, copy in self.items:
            if cond is None:
                copy.wait_send()
            else:
                pl.when(cond)(copy.wait_send)


def remote(src, dst, send, recv, device):
    return pltpu.make_async_remote_copy(
        src_ref=src, dst_ref=dst, send_sem=send, recv_sem=recv, device_id=device, device_id_type=MESH
    )


class Reduce:
    @staticmethod
    def sizes(n, side, depth):
        half = n // 2
        xq = half // side
        yq = xq // side
        tiles = yq // 8
        zr = 8 * -(-tiles // depth)
        return half, xq, yq, zr

    @staticmethod
    def scratch(n, side, depth):
        half, xq, yq, zr = Reduce.sizes(n, side, depth)
        dma = pltpu.SemaphoreType.DMA
        return [
            pltpu.VMEM((n, CH), BF),
            pltpu.VMEM((half, CH), BF),
            pltpu.VMEM((half, CH), BF),
            pltpu.VMEM((side - 1, xq, CH), BF),
            pltpu.VMEM((xq, CH), F32),
            pltpu.VMEM((side - 1, yq, CH), F32),
            pltpu.VMEM((yq, CH), F32),
            pltpu.VMEM((depth, zr, CH), F32),
            pltpu.VMEM((yq, CH), F32),
            pltpu.VMEM((xq, CH), F32),
            pltpu.VMEM((xq, CH), BF),
            pltpu.VMEM((half, CH), BF),
            pltpu.VMEM((n, CH), BF),
            dma((4, 4)),
            dma((4, 4)),
            dma((4,)),
            dma((4,)),
            dma((2, depth)),
            dma((2, depth)),
        ]

    def __init__(self, n, place, sent, refs):
        self.n, self.p, self.sent = n, place, sent
        self.half, self.xq, self.yq, self.zr = Reduce.sizes(n, place.side, place.depth)
        self.owners = self.yq // self.zr
        (self.src, self.rc, self.s1, self.rx, self.s2, self.ry, self.s3, self.rz, self.g3, self.g2,
         self.g2b, self.g1, self.fin, self.ssem, self.rsem, self.csend, self.crecv, self.zsend,
         self.zrecv) = refs
        self.waits = []

    def rows(self, index, size):
        return pl.ds(pl.multiple_of(index * size, 8), size)

    def rows16(self, index, size):
        return pl.ds(pl.multiple_of(index * size, 16), size)

    def _wait(self):
        for copy in self.waits:
            copy.wait_recv()
        self.waits = []

    def _send(self, src, dst, send, recv, device):
        copy = remote(src, dst, send, recv, device)
        self.sent.start(None, copy)
        self.waits.append(copy)

    def core_start(self):
        p = self.p
        self._send(self.src.at[self.rows16(1 - p.k, self.half)], self.rc, self.csend.at[0], self.crecv.at[0], p.at_core())

    def core_add(self):
        self._wait()
        own = self.rows16(self.p.k, self.half)
        self.s1[...] = (self.src[own, :].astype(F32) + self.rc[...].astype(F32)).astype(BF)

    def x_start(self):
        p = self.p
        for o in range(1, p.side):
            other = (p.x + o) % p.side
            self._send(self.s1.at[self.rows16(other, self.xq)], self.rx.at[o - 1], self.ssem.at[0, o], self.rsem.at[0, o], p.at_x(o))

    def x_add(self):
        self._wait()
        total = self.s1[self.rows16(self.p.x, self.xq), :].astype(F32)
        for o in range(1, self.p.side):
            total = total + self.rx[o - 1].astype(F32)
        self.s2[...] = total

    def y_start(self):
        p = self.p
        for o in range(1, p.side):
            other = (p.y + o) % p.side
            self._send(self.s2.at[self.rows(other, self.yq)], self.ry.at[o - 1], self.ssem.at[1, o], self.rsem.at[1, o], p.at_y(o))

    def y_add(self):
        self._wait()
        total = self.s2[self.rows(self.p.y, self.yq), :]
        for o in range(1, self.p.side):
            total = total + self.ry[o - 1]
        self.s3[...] = total

    def _z_out(self, o):
        p = self.p
        z = (p.z + o) % p.depth
        return z, remote(self.s3.at[self.rows(z, self.zr)], self.rz.at[o], self.zsend.at[0, o], self.zrecv.at[0, o], p.at_z(z))

    def z_start(self):
        def body(o, _):
            z = (self.p.z + o) % self.p.depth

            @pl.when(z < self.owners)
            def _():
                self._z_out(o)[1].start()

            return 0

        lax.fori_loop(1, self.p.depth, body, 0)

    def z_add(self):
        p = self.p

        @pl.when(p.z < self.owners)
        def _():
            def wait(o, _):
                remote(self.rz.at[o], self.rz.at[o], self.zsend.at[0, o], self.zrecv.at[0, o], p.at_z(p.z)).wait_recv()
                return 0

            lax.fori_loop(1, p.depth, wait, 0)
            own = self.rows(p.z, self.zr)
            total = self.s3[own, :]
            for o in range(1, p.depth):
                total = total + self.rz[o]
            self.g3[own, :] = total

    def _z_back(self, o):
        p = self.p
        z = (p.z + o) % p.depth
        own = self.g3.at[self.rows(p.z, self.zr)]
        return remote(own, own, self.zsend.at[1, o], self.zrecv.at[1, p.z], p.at_z(z))

    def zg_start(self):
        p = self.p

        @pl.when(p.z < self.owners)
        def _():
            def body(o, _):
                self._z_back(o).start()
                return 0

            lax.fori_loop(1, p.depth, body, 0)

    def zg_wait(self):
        p = self.p

        def body(z, _):
            @pl.when(z != p.z)
            def _():
                part = self.g3.at[self.rows(z, self.zr)]
                remote(part, part, self.zsend.at[1, z], self.zrecv.at[1, z], p.at_z(z)).wait_recv()

            return 0

        lax.fori_loop(0, self.owners, body, 0)

    def yg_start(self):
        p = self.p
        own = self.rows(p.y, self.yq)
        for o in range(1, p.side):
            copy = remote(self.g3, self.g2.at[own], self.ssem.at[2, o], self.rsem.at[2, o], p.at_y(o))
            self.sent.start(None, copy)
            other = self.rows((p.y + p.side - o) % p.side, self.yq)
            self.waits.append(remote(self.g3, self.g2.at[other], self.ssem.at[2, o], self.rsem.at[2, o], p.at_y(o)))
        self.g2[own, :] = self.g3[...]

    def xg_start(self):
        self._wait()
        p = self.p
        self.g2b[...] = self.g2[...].astype(BF)
        own = self.rows16(p.x, self.xq)
        for o in range(1, p.side):
            copy = remote(self.g2b, self.g1.at[own], self.ssem.at[3, o], self.rsem.at[3, o], p.at_x(o))
            self.sent.start(None, copy)
            other = self.rows16((p.x + p.side - o) % p.side, self.xq)
            self.waits.append(remote(self.g2b, self.g1.at[other], self.ssem.at[3, o], self.rsem.at[3, o], p.at_x(o)))
        self.g1[own, :] = self.g2b[...]

    def cg_start(self):
        self._wait()
        p = self.p
        own = self.rows16(p.k, self.half)
        other = self.rows16(1 - p.k, self.half)
        self.sent.start(None, remote(self.g1, self.fin.at[own], self.csend.at[1], self.crecv.at[1], p.at_core()))
        self.waits.append(remote(self.g1, self.fin.at[other], self.csend.at[1], self.crecv.at[1], p.at_core()))
        self.fin[own, :] = self.g1[...]

    def done(self):
        self._wait()

    def finish_sends(self):
        def body(o, _):
            z = (self.p.z + o) % self.p.depth

            @pl.when(z < self.owners)
            def _():
                self._z_out(o)[1].wait_send()

            @pl.when(self.p.z < self.owners)
            def _():
                self._z_back(o).wait_send()

            return 0

        lax.fori_loop(1, self.p.depth, body, 0)


def kernel(rows, cols, *refs):
    (contact, cotangent, conv_w, proj_w, out_map, out_sum,
     own, grad, wf, wb, pw, hid, hslope, mid, slope, sh, wide, rim, left, right, pack, mir, flat, acc, accp,
     hsend, hrecv, passing, msend, mrecv, psend, precv, mloc, loc) = refs[:34]
    p = Place(rows, cols)
    sent = Sent()
    per = (len(refs) - 34) // len(GROUPS)
    reduces = []
    for index, blocks in enumerate(GROUPS):
        start = 34 + index * per
        reduces.append(Reduce(len(blocks) * BLOCK_ROWS, p, sent, refs[start : start + per]))

    barrier = pltpu.get_barrier_semaphore()

    def greet(device):
        pl.semaphore_signal(barrier, inc=1, device_id=device, device_id_type=MESH)

    count = jnp.int32(1 + 2 * (p.side - 1) + p.depth - 1)
    greet(p.at_core())
    for o in range(1, p.side):
        greet(p.at_x(o))
        greet(p.at_y(o))

    def greet_z(o, _):
        greet(p.at_z((p.z + o) % p.depth))
        return 0

    lax.fori_loop(1, p.depth, greet_z, 0)
    for dr, dc in MOVES:
        there = p.inside(dr, dc)
        pl.when(there)(functools.partial(greet, (p.r + dr, p.c + dc)))
        count = count + there.astype(jnp.int32)
    apart, turned, swapped = p.q != p.r, p.x != p.y, p.zh != p.zl
    for h in range(2):
        pl.when(apart)(functools.partial(greet, (p.q, 2 * p.r + h)))
        pl.when(swapped)(functools.partial(greet, (p.zh * p.side + p.y, p.zl * 2 * p.side + 2 * p.x + h)))
        count = count + apart.astype(jnp.int32) + swapped.astype(jnp.int32)
    pl.when(turned)(functools.partial(greet, (p.zl * p.side + p.x, p.zh * 2 * p.side + 2 * p.y + p.k)))
    count = count + turned.astype(jnp.int32)

    loads = [
        pltpu.make_async_copy(contact, own, loc.at[0]),
        pltpu.make_async_copy(cotangent, grad, loc.at[1]),
        pltpu.make_async_copy(conv_w, wf, loc.at[2]),
        pltpu.make_async_copy(proj_w, pw, loc.at[3]),
    ]
    for load in loads:
        load.start()
    pl.semaphore_wait(barrier, count)

    half = CELLS // 2
    piece = half // PIECES
    by_relay = (p.x != p.y) & (p.zh != p.zl)
    mirrored = (p.q, 2 * p.r)
    relay = (p.zl * p.side + p.x, p.zh * 2 * p.side + 2 * p.y + p.k)
    beyond = (p.zh * p.side + p.y, p.zl * 2 * p.side + 2 * p.x)
    every = [(h, n) for n in range(PIECES) for h in range(2)]
    odd = [(h, n) for h, n in every if n % 2 == 1]

    def part_of(n):
        return pl.ds(n * piece, piece)

    def direct(turn, source, h, n):
        src = source.at[pl.ds(h * half + n * piece, piece)]
        dst = mir.at[turn, p.k, part_of(n)]
        device = (mirrored[0], mirrored[1] + h)
        return remote(src, dst, msend.at[turn, h, n], mrecv.at[turn, p.k, n], device)

    def staying(turn, source, n):
        src = source.at[pl.ds(p.k * half + n * piece, piece)]
        return pltpu.make_async_copy(src, mir.at[turn, p.k, part_of(n)], mloc.at[turn, n])

    def to_relay(turn, source, h, n):
        src = source.at[pl.ds(h * half + n * piece, piece)]
        return remote(src, passing.at[turn, h, part_of(n)], msend.at[turn, h, n], precv.at[turn, h, n], relay)

    def from_relay(turn, h, n):
        dst = mir.at[turn, p.k, part_of(n)]
        device = (beyond[0], beyond[1] + h)
        return remote(passing.at[turn, h, part_of(n)], dst, psend.at[turn, h, n], mrecv.at[turn, p.k, n], device)

    same = p.q == p.r

    def mirror_first(turn, source):
        for h, n in odd:
            sent.start(by_relay, to_relay(turn, source, h, n))

    def mirror_direct(turn, source, pieces):
        for h, n in pieces:
            stays = same & (p.k == h)
            goes = jnp.logical_not(stays)
            if n % 2 == 1:
                goes = goes & jnp.logical_not(by_relay)
            sent.start(goes, direct(turn, source, h, n))
            pl.when(stays)(staying(turn, source, n).start)

    def mirror_forward(turn, source):
        for h, n in odd:
            pl.when(by_relay)(to_relay(turn, source, h, n).wait_recv)
            sent.start(by_relay, from_relay(turn, h, n))

    def mirror_wait(turn, source):
        for h, n in every:
            stays = same & (p.k == h)
            arrives = remote(mir.at[turn, h, part_of(n)], mir.at[turn, h, part_of(n)], msend.at[turn, h, n],
                             mrecv.at[turn, h, n], (mirrored[0], mirrored[1] + h))
            pl.when(jnp.logical_not(stays))(arrives.wait_recv)
            pl.when(stays)(staying(turn, source, n).wait)

    def mirror_spread(turn):
        steps = half // CHUNK

        def body(i, _):
            flat[pl.ds(pl.multiple_of(i * CHUNK, CHUNK), CHUNK), :] = mir[
                turn, i // steps, pl.ds(pl.multiple_of((i % steps) * CHUNK, CHUNK), CHUNK), :
            ].astype(F32)
            return 0

        lax.fori_loop(0, CELLS // CHUNK, body, 0)

    def mirror_rows(chunk):
        base = (chunk // (COLS // STEP)) * half + (chunk % (COLS // STEP)) * STEP
        return jnp.concatenate([flat[pl.ds(base + j, COLS, stride=COLS), :] for j in range(STEP)], axis=0)

    mirror_first(0, contact)
    mirror_direct(0, contact, every)
    mirror_forward(0, contact)

    zero = functools.partial(jnp.zeros, dtype=BF)

    def fill(dr, dc, ref, at, shape):
        @pl.when(jnp.logical_not(p.inside(dr, dc)))
        def _():
            def body(e, _):
                ref[(e, *at)] = zero(shape)
                return 0

            lax.fori_loop(0, 2 * BLOCKS, body, 0)

    strip = MARGIN * COLS
    fill(-1, 0, sh, (1, pl.ds(0, strip)), (strip, CH))
    fill(1, 0, sh, (1, pl.ds((MARGIN + ROWS) * COLS, strip)), (strip, CH))
    for dc, ref in ((-1, left), (1, right)):
        fill(-1, dc, ref, (slice(None), pl.ds(0, CORNER)), (MARGIN, CORNER, CH))
        fill(0, dc, ref, (slice(None), pl.ds(CORNER, ROWS)), (MARGIN, ROWS, CH))
        fill(1, dc, ref, (slice(None), pl.ds(CORNER + ROWS, CORNER)), (MARGIN, CORNER, CH))

    loads[2].wait()
    loads[3].wait()

    def flip(index, _):
        block, tap = index // TAPS, index % TAPS
        tile = wf[block, pl.ds(pl.multiple_of(tap * CH, CH), CH), :].astype(F32)
        wb[block, pl.ds(pl.multiple_of((TAPS - 1 - tap) * CH, CH), CH), :] = tile.T.astype(BF)
        return 0

    lax.fori_loop(0, BLOCKS * TAPS, flip, 0)
    loads[0].wait()
    loads[1].wait()

    def cells(chunk):
        return pl.ds(pl.multiple_of(chunk * CHUNK, CHUNK), CHUNK)

    def put_center(e, chunk, values):
        rounded = values.astype(BF)
        sh[e, 1, pl.ds(pl.multiple_of(chunk * CHUNK + MARGIN * COLS, MARGIN * COLS), CHUNK), :] = rounded
        cube = values.reshape(STEP, COLS, CH)
        wide[pl.ds(chunk * STEP + MARGIN, STEP), MARGIN : MARGIN + COLS, :] = cube
        edge = STEP * MARGIN
        at = pl.ds(pl.multiple_of(chunk * edge, edge), edge)
        rim[0, at, :] = cube[:, :MARGIN, :].reshape(edge, CH)
        rim[1, at, :] = cube[:, COLS - MARGIN :, :].reshape(edge, CH)

    def halo_copy(e, d, index):
        dr, dc = MOVES[index]
        strip = d * COLS
        side = (dc + 1) // 2
        margin = right if dc < 0 else left
        if dr == 0:
            src = pack.at[e, side, pl.ds(0, d)]
            dst = margin.at[e, pl.ds(0, d), pl.ds(CORNER, ROWS)]
        elif dc == 0:
            start, end = (MARGIN, MARGIN + ROWS) if dr < 0 else (MARGIN + ROWS - d, MARGIN - d)
            src = sh.at[e, 1, pl.ds(start * COLS, strip)]
            dst = sh.at[e, 1, pl.ds(end * COLS, strip)]
        else:
            src = pack.at[e, side, pl.ds(0, d), pl.ds(0 if dr < 0 else ROWS - CORNER, CORNER)]
            dst = margin.at[e, pl.ds(0, d), pl.ds(CORNER + ROWS if dr < 0 else 0, CORNER)]
        return remote(src, dst, hsend.at[e, index], hrecv.at[e, index], (p.r + dr, p.c + dc))

    def halo_start(e, d):
        for j in range(d):
            pack[e, 0, j, :, :] = rim[0, pl.ds(j, ROWS, stride=MARGIN), :].astype(BF)
            pack[e, 1, j, :, :] = rim[1, pl.ds(MARGIN - d + j, ROWS, stride=MARGIN), :].astype(BF)
        for index, (dr, dc) in enumerate(MOVES):
            sent.start(p.inside(dr, dc), halo_copy(e, d, index))

    def halo_wait(e, d):
        for index, (dr, dc) in enumerate(MOVES):
            pl.when(p.inside(-dr, -dc))(halo_copy(e, d, index).wait_recv)

    def halo_build(e, d):
        for j in range(d):
            inner = CORNER - MARGIN
            rim[0, pl.ds(MARGIN - d + j, HIGH, stride=MARGIN), :] = left[e, j, :, :].astype(F32)[inner : inner + HIGH]
            rim[1, pl.ds(j, HIGH, stride=MARGIN), :] = right[e, j, :, :].astype(F32)[inner : inner + HIGH]
        wide[:, :MARGIN, :] = rim[0].reshape(HIGH, MARGIN, CH)
        wide[:, MARGIN + COLS :, :] = rim[1].reshape(HIGH, MARGIN, CH)
        for start in (MARGIN - d, MARGIN + ROWS):
            edge = sh[e, 1, start * COLS : (start + d) * COLS, :].astype(F32)
            wide[start : start + d, MARGIN : MARGIN + COLS, :] = edge.reshape(d, COLS, CH)

        def shift(i, _):
            first = MARGIN - d + 4 * i
            for b in (0, 2):
                begin = MARGIN + (b - 1) * d
                moved = wide[pl.ds(first, 4), begin : begin + COLS, :]
                sh[e, b, pl.ds(pl.multiple_of(first * COLS, 2 * COLS), 4 * COLS), :] = moved.reshape(4 * COLS, CH).astype(BF)
            return 0

        lax.fori_loop(0, (ROWS + 2 * d) // 4, shift, 0)

    def windows(e, d, chunk):
        taps = []
        for a in range(3):
            start = pl.multiple_of(chunk * CHUNK + (MARGIN + (a - 1) * d) * COLS, 2 * COLS)
            for b in range(3):
                taps.append(sh[e, b, pl.ds(start, CHUNK), :])
        return jnp.concatenate(taps, axis=1)

    def each_chunk(body):
        def run(chunk, _):
            body(chunk)
            return 0

        lax.fori_loop(0, CHUNKS, run, 0)

    mirror_wait(0, contact)
    mirror_spread(0)

    def first(chunk):
        at = cells(chunk)
        hidden = (0.5 * (own[at, :].astype(F32) + mirror_rows(chunk))).astype(BF)
        hid[0, at, :] = hidden
        act, steep = gelu_parts(hidden.astype(F32))
        hslope[0, at, :] = steep
        put_center(0, chunk, act)

    each_chunk(first)

    for k in range(BLOCKS):
        d = 2 ** (k + 1)
        halo_start(k, d)
        halo_wait(k, d)
        halo_build(k, d)

        def forward(chunk, k=k, d=d):
            at = cells(chunk)
            middle, steep = gelu_parts(dot(windows(k, d, chunk), wf[k]))
            middle = middle.astype(BF)
            mid[k, at, :] = middle
            slope[k, at, :] = steep
            if k + 1 < BLOCKS:
                hidden = (hid[k, at, :].astype(F32) + dot(middle, pw[k])).astype(BF)
                hid[k + 1, at, :] = hidden
                act, bend = gelu_parts(hidden.astype(F32))
                hslope[k + 1, at, :] = bend
                put_center(k + 1, chunk, act)
            else:
                put_center(k + 1, chunk, dot_nt(grad[at, :], pw[k]) * steep)

        each_chunk(forward)

    queues = []

    def advance(steps):
        for queue in queues * steps:
            if queue:
                queue.pop(0)()

    def phases(red):
        def both(a, b):
            def run():
                a()
                b()

            return run

        return [
            red.core_start,
            both(red.core_add, red.x_start),
            both(red.x_add, red.y_start),
            both(red.y_add, red.z_start),
            both(red.z_add, red.zg_start),
            both(red.zg_wait, red.yg_start),
            red.xg_start,
            red.cg_start,
            red.done,
        ]

    for k in reversed(range(BLOCKS)):
        d = 2 ** (k + 1)
        e = 2 * BLOCKS - 1 - k
        halo_start(e, d)
        acc[...] = jnp.zeros_like(acc)
        accp[...] = jnp.zeros_like(accp)

        def weights(chunk, k=k, d=d, e=e):
            at = cells(chunk)
            back = sh[e, 1, pl.ds(pl.multiple_of(chunk * CHUNK + MARGIN * COLS, MARGIN * COLS), CHUNK), :]
            acc[...] += dot_tn(back, windows(k, d, chunk))
            accp[...] += dot_tn(mid[k, at, :], grad[at, :])

        each_chunk(weights)
        group = next(i for i, blocks in enumerate(GROUPS) if k in blocks)
        base = GROUPS[group].index(k) * BLOCK_ROWS
        red = reduces[group]
        for tap in range(TAPS):
            red.src[base + tap * CH : base + (tap + 1) * CH, :] = acc[:, tap * CH : (tap + 1) * CH].T.astype(BF)
        red.src[base + TAPS * CH : base + BLOCK_ROWS, :] = accp[...].astype(BF)
        if k == GROUPS[group][-1]:
            queues.append(phases(red))
        advance(1)
        halo_wait(e, d)
        halo_build(e, d)

        def backward(chunk, k=k, d=d, e=e):
            at = cells(chunk)
            change = dot(windows(e, d, chunk), wb[k]) * hslope[k, at, :]
            new = (grad[at, :].astype(F32) + change).astype(BF)
            grad[at, :] = new
            if k > 0:
                put_center(e + 1, chunk, dot_nt(new, pw[k - 1]) * slope[k - 1, at, :])

        each_chunk(backward)
        advance(1)

    mirror_first(1, grad)
    mirror_direct(1, grad, every[:EARLY])
    mirror_forward(1, grad)
    advance(1)
    mirror_direct(1, grad, every[EARLY:])
    while any(queues):
        advance(1)
    for group, blocks in enumerate(GROUPS):
        for place, k in enumerate(blocks):
            base = place * BLOCK_ROWS
            fin = reduces[group].fin
            out_sum[k * TAPS * CH : (k + 1) * TAPS * CH, :] = fin[base : base + TAPS * CH, :]
            out_sum[CONV_ROWS + k * CH : CONV_ROWS + (k + 1) * CH, :] = fin[base + TAPS * CH : base + BLOCK_ROWS, :]
    mirror_wait(1, grad)
    mirror_spread(1)

    def last(chunk):
        at = cells(chunk)
        out_map[at, :] = (0.5 * (grad[at, :].astype(F32) + mirror_rows(chunk))).astype(BF)

    each_chunk(last)
    sent.finish()
    for red in reduces:
        red.finish_sends()


def solution(mesh):
    rows, cols = mesh.shape["row"], mesh.shape["col"]
    side = 4 if rows >= 16 else 2
    depth = (rows // side) * (cols // (2 * side))
    vmem, dma = pltpu.VMEM, pltpu.SemaphoreType.DMA
    scratch = [
        vmem((CELLS, CH), BF),
        vmem((CELLS, CH), BF),
        vmem((BLOCKS, TAPS * CH, CH), BF),
        vmem((BLOCKS, TAPS * CH, CH), BF),
        vmem((BLOCKS, CH, CH), BF),
        vmem((BLOCKS, CELLS, CH), BF),
        vmem((BLOCKS, CELLS, CH), F32),
        vmem((BLOCKS, CELLS, CH), BF),
        vmem((BLOCKS, CELLS, CH), F32),
        vmem((2 * BLOCKS, 3, HIGH * COLS, CH), BF),
        vmem((HIGH, WIDE, CH), F32),
        vmem((2, HIGH * MARGIN, CH), F32),
        vmem((2 * BLOCKS, MARGIN, TALL, CH), BF),
        vmem((2 * BLOCKS, MARGIN, TALL, CH), BF),
        vmem((2 * BLOCKS, 2, MARGIN, ROWS, CH), BF),
        vmem((2, 2, CELLS // 2, CH), BF),
        vmem((CELLS, CH), F32),
        vmem((CH, TAPS * CH), F32),
        vmem((CH, CH), F32),
        dma((2 * BLOCKS, 8)),
        dma((2 * BLOCKS, 8)),
        vmem((2, 2, CELLS // 2, CH), BF),
        dma((2, 2, PIECES)),
        dma((2, 2, PIECES)),
        dma((2, 2, PIECES)),
        dma((2, 2, PIECES)),
        dma((2, PIECES)),
        dma((4,)),
    ]
    for blocks in GROUPS:
        scratch += Reduce.scratch(len(blocks) * BLOCK_ROWS, side, depth)

    scale = 1.0 / (rows * ROWS)

    def body(contact_map, cotangent, conv_weight, proj_weight):
        out_map, out_sum = pl.pallas_call(
            functools.partial(kernel, rows, cols),
            out_shape=(
                jax.ShapeDtypeStruct((CELLS, CH), BF),
                jax.ShapeDtypeStruct((BLOCKS * BLOCK_ROWS, CH), BF),
            ),
            in_specs=[pl.BlockSpec(memory_space=pl.ANY)] * 4,
            out_specs=(pl.BlockSpec(memory_space=pltpu.VMEM),) * 2,
            scratch_shapes=scratch,
            compiler_params=pltpu.CompilerParams(
                collective_id=0, has_side_effects=True, vmem_limit_bytes=56 * 1024 * 1024
            ),
        )(
            contact_map.reshape(CELLS, CH),
            cotangent.reshape(CELLS, CH),
            conv_weight.reshape(BLOCKS, TAPS * CH, CH),
            proj_weight,
        )
        return (
            out_map.reshape(ROWS, COLS, CH),
            (out_sum[:CONV_ROWS].astype(F32) * scale).reshape(BLOCKS, 3, 3, CH, CH),
            (out_sum[CONV_ROWS:].astype(F32) * scale).reshape(BLOCKS, CH, CH),
        )

    in_specs = (P("row", "col", None), P("row", "col", None), P(), P())
    out_specs = (P("row", "col", None), P(), P())
    return jax.shard_map(body, mesh=mesh, in_specs=in_specs, out_specs=out_specs, check_vma=False)
```

```python
import functools

import jax
import jax.numpy as jnp
from jax import lax
from jax.experimental import pallas as pl
from jax.experimental.pallas import tpu as pltpu
from jax.sharding import PartitionSpec as P

MESH = pl.DeviceIdType.MESH
BF = jnp.bfloat16
F32 = jnp.float32
ROWS, COLS, CH, MARGIN = 64, 32, 128, 8
CELLS = ROWS * COLS
CORNER = 16
TALL = ROWS + 2 * CORNER
HIGH, WIDE = ROWS + 2 * MARGIN, COLS + 2 * MARGIN
STEP = 32
CHUNK = STEP * COLS
CHUNKS = ROWS // STEP
TAPS = 9
BLOCKS = 3
SLOPE_C = 0.7978845608028654
CUBIC = 0.044715
MOVES = ((-1, -1), (-1, 1), (1, -1), (1, 1), (0, -1), (0, 1), (-1, 0), (1, 0))
GROUPS = ((2, 1, 0),)
BLOCK_ROWS = (TAPS + 1) * CH
PIECES = 4
EARLY = 4
CONV_ROWS = BLOCKS * TAPS * CH


def gelu_parts(v):
    u = v * v
    t = jnp.tanh(SLOPE_C * v * (1.0 + CUBIC * u))
    half = 0.5 + 0.5 * t
    slope = half + (0.5 * SLOPE_C) * v * (1.0 - t * t) * (1.0 + 3.0 * CUBIC * u)
    return v * half, slope


def dot(a, b):
    return jnp.dot(a, b, preferred_element_type=F32)


def dot_nt(a, b):
    return lax.dot_general(a, b, (((1,), (1,)), ((), ())), preferred_element_type=F32)


def dot_tn(a, b):
    return lax.dot_general(a, b, (((0,), (0,)), ((), ())), preferred_element_type=F32)


class Place:
    def __init__(self, rows, cols):
        self.rows, self.cols = rows, cols
        self.side = 4 if rows >= 16 else 2
        self.depth = (rows // self.side) * (cols // (2 * self.side))
        self.parts = rows // self.side
        self.r, self.c = lax.axis_index("row"), lax.axis_index("col")
        self.y, self.zl = self.r % self.side, self.r // self.side
        self.k = self.c % 2
        self.q = self.c // 2
        self.x, self.zh = self.q % self.side, self.q // self.side
        self.z = self.zh * self.parts + self.zl

    def at_core(self):
        return (self.r, self.c + 1 - 2 * self.k)

    def at_x(self, offset):
        x = (self.x + offset) % self.side
        return (self.r, self.zh * 2 * self.side + 2 * x + self.k)

    def at_y(self, offset):
        y = (self.y + offset) % self.side
        return (self.zl * self.side + y, self.c)

    def at_z(self, z):
        zh, zl = z // self.parts, z % self.parts
        return (zl * self.side + self.y, zh * 2 * self.side + 2 * self.x + self.k)

    def inside(self, dr, dc):
        r, c = self.r + dr, self.c + dc
        return (r >= 0) & (r < self.rows) & (c >= 0) & (c < self.cols)


class Sent:
    def __init__(self):
        self.items = []

    def start(self, cond, copy):
        if cond is None:
            copy.start()
        else:
            pl.when(cond)(copy.start)
        self.items.append((cond, copy))

    def finish(self):
        for cond, copy in self.items:
            if cond is None:
                copy.wait_send()
            else:
                pl.when(cond)(copy.wait_send)


def remote(src, dst, send, recv, device):
    return pltpu.make_async_remote_copy(
        src_ref=src, dst_ref=dst, send_sem=send, recv_sem=recv, device_id=device, device_id_type=MESH
    )


class Reduce:
    @staticmethod
    def sizes(n, side, depth):
        half = n // 2
        xq = half // side
        yq = xq // side
        tiles = yq // 8
        zr = 8 * -(-tiles // depth)
        return half, xq, yq, zr

    @staticmethod
    def scratch(n, side, depth):
        half, xq, yq, zr = Reduce.sizes(n, side, depth)
        dma = pltpu.SemaphoreType.DMA
        return [
            pltpu.VMEM((n, CH), BF),
            pltpu.VMEM((half, CH), BF),
            pltpu.VMEM((half, CH), BF),
            pltpu.VMEM((side - 1, xq, CH), BF),
            pltpu.VMEM((xq, CH), F32),
            pltpu.VMEM((side - 1, yq, CH), F32),
            pltpu.VMEM((yq, CH), F32),
            pltpu.VMEM((depth, zr, CH), F32),
            pltpu.VMEM((yq, CH), F32),
            pltpu.VMEM((xq, CH), F32),
            pltpu.VMEM((xq, CH), BF),
            pltpu.VMEM((half, CH), BF),
            pltpu.VMEM((n, CH), BF),
            dma((4, 4)),
            dma((4, 4)),
            dma((4,)),
            dma((4,)),
            dma((2, depth)),
            dma((2, depth)),
        ]

    def __init__(self, n, place, sent, refs):
        self.n, self.p, self.sent = n, place, sent
        self.half, self.xq, self.yq, self.zr = Reduce.sizes(n, place.side, place.depth)
        self.owners = self.yq // self.zr
        (self.src, self.rc, self.s1, self.rx, self.s2, self.ry, self.s3, self.rz, self.g3, self.g2,
         self.g2b, self.g1, self.fin, self.ssem, self.rsem, self.csend, self.crecv, self.zsend,
         self.zrecv) = refs
        self.waits = []

    def rows(self, index, size):
        return pl.ds(pl.multiple_of(index * size, 8), size)

    def rows16(self, index, size):
        return pl.ds(pl.multiple_of(index * size, 16), size)

    def _wait(self):
        for copy in self.waits:
            copy.wait_recv()
        self.waits = []

    def _send(self, src, dst, send, recv, device):
        copy = remote(src, dst, send, recv, device)
        self.sent.start(None, copy)
        self.waits.append(copy)

    def core_start(self):
        p = self.p
        self._send(self.src.at[self.rows16(1 - p.k, self.half)], self.rc, self.csend.at[0], self.crecv.at[0], p.at_core())

    def core_add(self):
        self._wait()
        own = self.rows16(self.p.k, self.half)
        self.s1[...] = (self.src[own, :].astype(F32) + self.rc[...].astype(F32)).astype(BF)

    def x_start(self):
        p = self.p
        for o in range(1, p.side):
            other = (p.x + o) % p.side
            self._send(self.s1.at[self.rows16(other, self.xq)], self.rx.at[o - 1], self.ssem.at[0, o], self.rsem.at[0, o], p.at_x(o))

    def x_add(self):
        self._wait()
        total = self.s1[self.rows16(self.p.x, self.xq), :].astype(F32)
        for o in range(1, self.p.side):
            total = total + self.rx[o - 1].astype(F32)
        self.s2[...] = total

    def y_start(self):
        p = self.p
        for o in range(1, p.side):
            other = (p.y + o) % p.side
            self._send(self.s2.at[self.rows(other, self.yq)], self.ry.at[o - 1], self.ssem.at[1, o], self.rsem.at[1, o], p.at_y(o))

    def y_add(self):
        self._wait()
        total = self.s2[self.rows(self.p.y, self.yq), :]
        for o in range(1, self.p.side):
            total = total + self.ry[o - 1]
        self.s3[...] = total

    def _z_out(self, o):
        p = self.p
        z = (p.z + o) % p.depth
        return z, remote(self.s3.at[self.rows(z, self.zr)], self.rz.at[o], self.zsend.at[0, o], self.zrecv.at[0, o], p.at_z(z))

    def z_start(self):
        def body(o, _):
            z = (self.p.z + o) % self.p.depth

            @pl.when(z < self.owners)
            def _():
                self._z_out(o)[1].start()

            return 0

        lax.fori_loop(1, self.p.depth, body, 0)

    def z_add(self):
        p = self.p

        @pl.when(p.z < self.owners)
        def _():
            def wait(o, _):
                remote(self.rz.at[o], self.rz.at[o], self.zsend.at[0, o], self.zrecv.at[0, o], p.at_z(p.z)).wait_recv()
                return 0

            lax.fori_loop(1, p.depth, wait, 0)
            own = self.rows(p.z, self.zr)
            total = self.s3[own, :]
            for o in range(1, p.depth):
                total = total + self.rz[o]
            self.g3[own, :] = total

    def _z_back(self, o):
        p = self.p
        z = (p.z + o) % p.depth
        own = self.g3.at[self.rows(p.z, self.zr)]
        return remote(own, own, self.zsend.at[1, o], self.zrecv.at[1, p.z], p.at_z(z))

    def zg_start(self):
        p = self.p

        @pl.when(p.z < self.owners)
        def _():
            def body(o, _):
                self._z_back(o).start()
                return 0

            lax.fori_loop(1, p.depth, body, 0)

    def zg_wait(self):
        p = self.p

        def body(z, _):
            @pl.when(z != p.z)
            def _():
                part = self.g3.at[self.rows(z, self.zr)]
                remote(part, part, self.zsend.at[1, z], self.zrecv.at[1, z], p.at_z(z)).wait_recv()

            return 0

        lax.fori_loop(0, self.owners, body, 0)

    def yg_start(self):
        p = self.p
        own = self.rows(p.y, self.yq)
        for o in range(1, p.side):
            copy = remote(self.g3, self.g2.at[own], self.ssem.at[2, o], self.rsem.at[2, o], p.at_y(o))
            self.sent.start(None, copy)
            other = self.rows((p.y + p.side - o) % p.side, self.yq)
            self.waits.append(remote(self.g3, self.g2.at[other], self.ssem.at[2, o], self.rsem.at[2, o], p.at_y(o)))
        self.g2[own, :] = self.g3[...]

    def xg_start(self):
        self._wait()
        p = self.p
        self.g2b[...] = self.g2[...].astype(BF)
        own = self.rows16(p.x, self.xq)
        for o in range(1, p.side):
            copy = remote(self.g2b, self.g1.at[own], self.ssem.at[3, o], self.rsem.at[3, o], p.at_x(o))
            self.sent.start(None, copy)
            other = self.rows16((p.x + p.side - o) % p.side, self.xq)
            self.waits.append(remote(self.g2b, self.g1.at[other], self.ssem.at[3, o], self.rsem.at[3, o], p.at_x(o)))
        self.g1[own, :] = self.g2b[...]

    def cg_start(self):
        self._wait()
        p = self.p
        own = self.rows16(p.k, self.half)
        other = self.rows16(1 - p.k, self.half)
        self.sent.start(None, remote(self.g1, self.fin.at[own], self.csend.at[1], self.crecv.at[1], p.at_core()))
        self.waits.append(remote(self.g1, self.fin.at[other], self.csend.at[1], self.crecv.at[1], p.at_core()))
        self.fin[own, :] = self.g1[...]

    def done(self):
        self._wait()

    def finish_sends(self):
        def body(o, _):
            z = (self.p.z + o) % self.p.depth

            @pl.when(z < self.owners)
            def _():
                self._z_out(o)[1].wait_send()

            @pl.when(self.p.z < self.owners)
            def _():
                self._z_back(o).wait_send()

            return 0

        lax.fori_loop(1, self.p.depth, body, 0)


def kernel(rows, cols, *refs):
    (contact, cotangent, conv_w, proj_w, out_map, out_sum,
     own, grad, wf, wb, pw, hid, hslope, mid, slope, sh, wide, rim, left, right, pack, mir, flat, acc, accp,
     hsend, hrecv, passing, msend, mrecv, psend, precv, mloc, loc) = refs[:34]
    p = Place(rows, cols)
    sent = Sent()
    per = (len(refs) - 34) // len(GROUPS)
    reduces = []
    for index, blocks in enumerate(GROUPS):
        start = 34 + index * per
        reduces.append(Reduce(len(blocks) * BLOCK_ROWS, p, sent, refs[start : start + per]))

    barrier = pltpu.get_barrier_semaphore()

    def greet(device):
        pl.semaphore_signal(barrier, inc=1, device_id=device, device_id_type=MESH)

    count = jnp.int32(1 + 2 * (p.side - 1) + p.depth - 1)
    greet(p.at_core())
    for o in range(1, p.side):
        greet(p.at_x(o))
        greet(p.at_y(o))

    def greet_z(o, _):
        greet(p.at_z((p.z + o) % p.depth))
        return 0

    lax.fori_loop(1, p.depth, greet_z, 0)
    for dr, dc in MOVES:
        there = p.inside(dr, dc)
        pl.when(there)(functools.partial(greet, (p.r + dr, p.c + dc)))
        count = count + there.astype(jnp.int32)
    apart, turned, swapped = p.q != p.r, p.x != p.y, p.zh != p.zl
    for h in range(2):
        pl.when(apart)(functools.partial(greet, (p.q, 2 * p.r + h)))
        pl.when(swapped)(functools.partial(greet, (p.zh * p.side + p.y, p.zl * 2 * p.side + 2 * p.x + h)))
        count = count + apart.astype(jnp.int32) + swapped.astype(jnp.int32)
    pl.when(turned)(functools.partial(greet, (p.zl * p.side + p.x, p.zh * 2 * p.side + 2 * p.y + p.k)))
    count = count + turned.astype(jnp.int32)

    loads = [
        pltpu.make_async_copy(contact, own, loc.at[0]),
        pltpu.make_async_copy(cotangent, grad, loc.at[1]),
        pltpu.make_async_copy(conv_w, wf, loc.at[2]),
        pltpu.make_async_copy(proj_w, pw, loc.at[3]),
    ]
    for load in loads:
        load.start()
    pl.semaphore_wait(barrier, count)

    half = CELLS // 2
    piece = half // PIECES
    by_relay = (p.x != p.y) & (p.zh != p.zl)
    mirrored = (p.q, 2 * p.r)
    relay = (p.zl * p.side + p.x, p.zh * 2 * p.side + 2 * p.y + p.k)
    beyond = (p.zh * p.side + p.y, p.zl * 2 * p.side + 2 * p.x)
    every = [(h, n) for n in range(PIECES) for h in range(2)]
    odd = [(h, n) for h, n in every if n % 2 == 1]

    def part_of(n):
        return pl.ds(n * piece, piece)

    def direct(turn, source, h, n):
        src = source.at[pl.ds(h * half + n * piece, piece)]
        dst = mir.at[turn, p.k, part_of(n)]
        device = (mirrored[0], mirrored[1] + h)
        return remote(src, dst, msend.at[turn, h, n], mrecv.at[turn, p.k, n], device)

    def staying(turn, source, n):
        src = source.at[pl.ds(p.k * half + n * piece, piece)]
        return pltpu.make_async_copy(src, mir.at[turn, p.k, part_of(n)], mloc.at[turn, n])

    def to_relay(turn, source, h, n):
        src = source.at[pl.ds(h * half + n * piece, piece)]
        return remote(src, passing.at[turn, h, part_of(n)], msend.at[turn, h, n], precv.at[turn, h, n], relay)

    def from_relay(turn, h, n):
        dst = mir.at[turn, p.k, part_of(n)]
        device = (beyond[0], beyond[1] + h)
        return remote(passing.at[turn, h, part_of(n)], dst, psend.at[turn, h, n], mrecv.at[turn, p.k, n], device)

    same = p.q == p.r

    def mirror_first(turn, source):
        for h, n in odd:
            sent.start(by_relay, to_relay(turn, source, h, n))

    def mirror_direct(turn, source, pieces):
        for h, n in pieces:
            stays = same & (p.k == h)
            goes = jnp.logical_not(stays)
            if n % 2 == 1:
                goes = goes & jnp.logical_not(by_relay)
            sent.start(goes, direct(turn, source, h, n))
            pl.when(stays)(staying(turn, source, n).start)

    def mirror_forward(turn, source):
        for h, n in odd:
            pl.when(by_relay)(to_relay(turn, source, h, n).wait_recv)
            sent.start(by_relay, from_relay(turn, h, n))

    def mirror_wait(turn, source):
        for h, n in every:
            stays = same & (p.k == h)
            arrives = remote(mir.at[turn, h, part_of(n)], mir.at[turn, h, part_of(n)], msend.at[turn, h, n],
                             mrecv.at[turn, h, n], (mirrored[0], mirrored[1] + h))
            pl.when(jnp.logical_not(stays))(arrives.wait_recv)
            pl.when(stays)(staying(turn, source, n).wait)

    def mirror_spread(turn):
        steps = half // CHUNK

        def body(i, _):
            flat[pl.ds(pl.multiple_of(i * CHUNK, CHUNK), CHUNK), :] = mir[
                turn, i // steps, pl.ds(pl.multiple_of((i % steps) * CHUNK, CHUNK), CHUNK), :
            ].astype(F32)
            return 0

        lax.fori_loop(0, CELLS // CHUNK, body, 0)

    def mirror_rows(chunk):
        base = (chunk // (COLS // STEP)) * half + (chunk % (COLS // STEP)) * STEP
        return jnp.concatenate([flat[pl.ds(base + j, COLS, stride=COLS), :] for j in range(STEP)], axis=0)

    mirror_first(0, contact)
    mirror_direct(0, contact, every)
    mirror_forward(0, contact)

    zero = functools.partial(jnp.zeros, dtype=BF)

    def fill(dr, dc, ref, at, shape):
        @pl.when(jnp.logical_not(p.inside(dr, dc)))
        def _():
            def body(e, _):
                ref[(e, *at)] = zero(shape)
                return 0

            lax.fori_loop(0, 2 * BLOCKS, body, 0)

    strip = MARGIN * COLS
    fill(-1, 0, sh, (1, pl.ds(0, strip)), (strip, CH))
    fill(1, 0, sh, (1, pl.ds((MARGIN + ROWS) * COLS, strip)), (strip, CH))
    for dc, ref in ((-1, left), (1, right)):
        fill(-1, dc, ref, (slice(None), pl.ds(0, CORNER)), (MARGIN, CORNER, CH))
        fill(0, dc, ref, (slice(None), pl.ds(CORNER, ROWS)), (MARGIN, ROWS, CH))
        fill(1, dc, ref, (slice(None), pl.ds(CORNER + ROWS, CORNER)), (MARGIN, CORNER, CH))

    loads[2].wait()
    loads[3].wait()

    def flip(index, _):
        block, tap = index // TAPS, index % TAPS
        tile = wf[block, pl.ds(pl.multiple_of(tap * CH, CH), CH), :].astype(F32)
        wb[block, pl.ds(pl.multiple_of((TAPS - 1 - tap) * CH, CH), CH), :] = tile.T.astype(BF)
        return 0

    lax.fori_loop(0, BLOCKS * TAPS, flip, 0)
    loads[0].wait()
    loads[1].wait()

    def cells(chunk):
        return pl.ds(pl.multiple_of(chunk * CHUNK, CHUNK), CHUNK)

    def put_center(e, chunk, values):
        rounded = values.astype(BF)
        sh[e, 1, pl.ds(pl.multiple_of(chunk * CHUNK + MARGIN * COLS, MARGIN * COLS), CHUNK), :] = rounded
        cube = values.reshape(STEP, COLS, CH)
        wide[pl.ds(chunk * STEP + MARGIN, STEP), MARGIN : MARGIN + COLS, :] = cube
        edge = STEP * MARGIN
        at = pl.ds(pl.multiple_of(chunk * edge, edge), edge)
        rim[0, at, :] = cube[:, :MARGIN, :].reshape(edge, CH)
        rim[1, at, :] = cube[:, COLS - MARGIN :, :].reshape(edge, CH)

    def halo_copy(e, d, index):
        dr, dc = MOVES[index]
        strip = d * COLS
        side = (dc + 1) // 2
        margin = right if dc < 0 else left
        if dr == 0:
            src = pack.at[e, side, pl.ds(0, d)]
            dst = margin.at[e, pl.ds(0, d), pl.ds(CORNER, ROWS)]
        elif dc == 0:
            start, end = (MARGIN, MARGIN + ROWS) if dr < 0 else (MARGIN + ROWS - d, MARGIN - d)
            src = sh.at[e, 1, pl.ds(start * COLS, strip)]
            dst = sh.at[e, 1, pl.ds(end * COLS, strip)]
        else:
            src = pack.at[e, side, pl.ds(0, d), pl.ds(0 if dr < 0 else ROWS - CORNER, CORNER)]
            dst = margin.at[e, pl.ds(0, d), pl.ds(CORNER + ROWS if dr < 0 else 0, CORNER)]
        return remote(src, dst, hsend.at[e, index], hrecv.at[e, index], (p.r + dr, p.c + dc))

    def halo_start(e, d):
        for j in range(d):
            pack[e, 0, j, :, :] = rim[0, pl.ds(j, ROWS, stride=MARGIN), :].astype(BF)
            pack[e, 1, j, :, :] = rim[1, pl.ds(MARGIN - d + j, ROWS, stride=MARGIN), :].astype(BF)
        for index, (dr, dc) in enumerate(MOVES):
            sent.start(p.inside(dr, dc), halo_copy(e, d, index))

    def halo_wait(e, d):
        for index, (dr, dc) in enumerate(MOVES):
            pl.when(p.inside(-dr, -dc))(halo_copy(e, d, index).wait_recv)

    def halo_build(e, d):
        for j in range(d):
            inner = CORNER - MARGIN
            rim[0, pl.ds(MARGIN - d + j, HIGH, stride=MARGIN), :] = left[e, j, :, :].astype(F32)[inner : inner + HIGH]
            rim[1, pl.ds(j, HIGH, stride=MARGIN), :] = right[e, j, :, :].astype(F32)[inner : inner + HIGH]
        wide[:, :MARGIN, :] = rim[0].reshape(HIGH, MARGIN, CH)
        wide[:, MARGIN + COLS :, :] = rim[1].reshape(HIGH, MARGIN, CH)
        for start in (MARGIN - d, MARGIN + ROWS):
            edge = sh[e, 1, start * COLS : (start + d) * COLS, :].astype(F32)
            wide[start : start + d, MARGIN : MARGIN + COLS, :] = edge.reshape(d, COLS, CH)

        def shift(i, _):
            first = MARGIN - d + 4 * i
            for b in (0, 2):
                begin = MARGIN + (b - 1) * d
                moved = wide[pl.ds(first, 4), begin : begin + COLS, :]
                sh[e, b, pl.ds(pl.multiple_of(first * COLS, 2 * COLS), 4 * COLS), :] = moved.reshape(4 * COLS, CH).astype(BF)
            return 0

        lax.fori_loop(0, (ROWS + 2 * d) // 4, shift, 0)

    def windows(e, d, chunk):
        taps = []
        for a in range(3):
            start = pl.multiple_of(chunk * CHUNK + (MARGIN + (a - 1) * d) * COLS, 2 * COLS)
            for b in range(3):
                taps.append(sh[e, b, pl.ds(start, CHUNK), :])
        return jnp.concatenate(taps, axis=1)

    def each_chunk(body):
        def run(chunk, _):
            body(chunk)
            return 0

        lax.fori_loop(0, CHUNKS, run, 0)

    mirror_wait(0, contact)
    mirror_spread(0)

    def first(chunk):
        at = cells(chunk)
        hidden = (0.5 * (own[at, :].astype(F32) + mirror_rows(chunk))).astype(BF)
        hid[0, at, :] = hidden
        act, steep = gelu_parts(hidden.astype(F32))
        hslope[0, at, :] = steep
        put_center(0, chunk, act)

    each_chunk(first)

    for k in range(BLOCKS):
        d = 2 ** (k + 1)
        halo_start(k, d)
        halo_wait(k, d)
        halo_build(k, d)

        def forward(chunk, k=k, d=d):
            at = cells(chunk)
            middle, steep = gelu_parts(dot(windows(k, d, chunk), wf[k]))
            middle = middle.astype(BF)
            mid[k, at, :] = middle
            slope[k, at, :] = steep
            if k + 1 < BLOCKS:
                hidden = (hid[k, at, :].astype(F32) + dot(middle, pw[k])).astype(BF)
                hid[k + 1, at, :] = hidden
                act, bend = gelu_parts(hidden.astype(F32))
                hslope[k + 1, at, :] = bend
                put_center(k + 1, chunk, act)
            else:
                put_center(k + 1, chunk, dot_nt(grad[at, :], pw[k]) * steep)

        each_chunk(forward)

    queues = []

    def advance(steps):
        for queue in queues * steps:
            if queue:
                queue.pop(0)()

    def phases(red):
        def both(a, b):
            def run():
                a()
                b()

            return run

        return [
            red.core_start,
            both(red.core_add, red.x_start),
            both(red.x_add, red.y_start),
            both(red.y_add, red.z_start),
            both(red.z_add, red.zg_start),
            both(red.zg_wait, red.yg_start),
            red.xg_start,
            red.cg_start,
            red.done,
        ]

    for k in reversed(range(BLOCKS)):
        d = 2 ** (k + 1)
        e = 2 * BLOCKS - 1 - k
        halo_start(e, d)
        acc[...] = jnp.zeros_like(acc)
        accp[...] = jnp.zeros_like(accp)

        def weights(chunk, k=k, d=d, e=e):
            at = cells(chunk)
            back = sh[e, 1, pl.ds(pl.multiple_of(chunk * CHUNK + MARGIN * COLS, MARGIN * COLS), CHUNK), :]
            acc[...] += dot_tn(back, windows(k, d, chunk))
            accp[...] += dot_tn(mid[k, at, :], grad[at, :])

        each_chunk(weights)
        group = next(i for i, blocks in enumerate(GROUPS) if k in blocks)
        base = GROUPS[group].index(k) * BLOCK_ROWS
        red = reduces[group]
        for tap in range(TAPS):
            red.src[base + tap * CH : base + (tap + 1) * CH, :] = acc[:, tap * CH : (tap + 1) * CH].T.astype(BF)
        red.src[base + TAPS * CH : base + BLOCK_ROWS, :] = accp[...].astype(BF)
        if k == GROUPS[group][-1]:
            queues.append(phases(red))
        advance(1)
        halo_wait(e, d)
        halo_build(e, d)

        def backward(chunk, k=k, d=d, e=e):
            at = cells(chunk)
            change = dot(windows(e, d, chunk), wb[k]) * hslope[k, at, :]
            new = (grad[at, :].astype(F32) + change).astype(BF)
            grad[at, :] = new
            if k > 0:
                put_center(e + 1, chunk, dot_nt(new, pw[k - 1]) * slope[k - 1, at, :])

        each_chunk(backward)
        advance(1)

    mirror_first(1, grad)
    mirror_direct(1, grad, every[:EARLY])
    mirror_forward(1, grad)
    advance(1)
    mirror_direct(1, grad, every[EARLY:])
    while any(len(queue) > 1 for queue in queues):
        advance(1)
    mirror_wait(1, grad)
    mirror_spread(1)

    def last(chunk):
        at = cells(chunk)
        out_map[at, :] = (0.5 * (grad[at, :].astype(F32) + mirror_rows(chunk))).astype(BF)

    each_chunk(last)
    advance(1)
    for group, blocks in enumerate(GROUPS):
        for place, k in enumerate(blocks):
            base = place * BLOCK_ROWS
            fin = reduces[group].fin
            out_sum[k * TAPS * CH : (k + 1) * TAPS * CH, :] = fin[base : base + TAPS * CH, :]
            out_sum[CONV_ROWS + k * CH : CONV_ROWS + (k + 1) * CH, :] = fin[base + TAPS * CH : base + BLOCK_ROWS, :]
    sent.finish()
    for red in reduces:
        red.finish_sends()


def solution(mesh):
    rows, cols = mesh.shape["row"], mesh.shape["col"]
    side = 4 if rows >= 16 else 2
    depth = (rows // side) * (cols // (2 * side))
    vmem, dma = pltpu.VMEM, pltpu.SemaphoreType.DMA
    scratch = [
        vmem((CELLS, CH), BF),
        vmem((CELLS, CH), BF),
        vmem((BLOCKS, TAPS * CH, CH), BF),
        vmem((BLOCKS, TAPS * CH, CH), BF),
        vmem((BLOCKS, CH, CH), BF),
        vmem((BLOCKS, CELLS, CH), BF),
        vmem((BLOCKS, CELLS, CH), F32),
        vmem((BLOCKS, CELLS, CH), BF),
        vmem((BLOCKS, CELLS, CH), F32),
        vmem((2 * BLOCKS, 3, HIGH * COLS, CH), BF),
        vmem((HIGH, WIDE, CH), F32),
        vmem((2, HIGH * MARGIN, CH), F32),
        vmem((2 * BLOCKS, MARGIN, TALL, CH), BF),
        vmem((2 * BLOCKS, MARGIN, TALL, CH), BF),
        vmem((2 * BLOCKS, 2, MARGIN, ROWS, CH), BF),
        vmem((2, 2, CELLS // 2, CH), BF),
        vmem((CELLS, CH), F32),
        vmem((CH, TAPS * CH), F32),
        vmem((CH, CH), F32),
        dma((2 * BLOCKS, 8)),
        dma((2 * BLOCKS, 8)),
        vmem((2, 2, CELLS // 2, CH), BF),
        dma((2, 2, PIECES)),
        dma((2, 2, PIECES)),
        dma((2, 2, PIECES)),
        dma((2, 2, PIECES)),
        dma((2, PIECES)),
        dma((4,)),
    ]
    for blocks in GROUPS:
        scratch += Reduce.scratch(len(blocks) * BLOCK_ROWS, side, depth)

    scale = 1.0 / (rows * ROWS)

    def body(contact_map, cotangent, conv_weight, proj_weight):
        out_map, out_sum = pl.pallas_call(
            functools.partial(kernel, rows, cols),
            out_shape=(
                jax.ShapeDtypeStruct((CELLS, CH), BF),
                jax.ShapeDtypeStruct((BLOCKS * BLOCK_ROWS, CH), BF),
            ),
            in_specs=[pl.BlockSpec(memory_space=pl.ANY)] * 4,
            out_specs=(pl.BlockSpec(memory_space=pltpu.VMEM),) * 2,
            scratch_shapes=scratch,
            compiler_params=pltpu.CompilerParams(
                collective_id=0, has_side_effects=True, vmem_limit_bytes=56 * 1024 * 1024
            ),
        )(
            contact_map.reshape(CELLS, CH),
            cotangent.reshape(CELLS, CH),
            conv_weight.reshape(BLOCKS, TAPS * CH, CH),
            proj_weight,
        )
        return (
            out_map.reshape(ROWS, COLS, CH),
            (out_sum[:CONV_ROWS].astype(F32) * scale).reshape(BLOCKS, 3, 3, CH, CH),
            (out_sum[CONV_ROWS:].astype(F32) * scale).reshape(BLOCKS, CH, CH),
        )

    in_specs = (P("row", "col", None), P("row", "col", None), P(), P())
    out_specs = (P("row", "col", None), P(), P())
    return jax.shard_map(body, mesh=mesh, in_specs=in_specs, out_specs=out_specs, check_vma=False)
```
